32 devices in a mesh: stream: 8 (over z, y), span: 4 (over x, core).
Axes of the slice: x: 2, y: 2, z: 4, core: 2. Of those that a mesh axis runs over, the one named last changes fastest.
Arguments:
- rhs: float32 [32, 4, 64, 4096], P('stream', None, None, 'span'), may hold values from -0.15625 to 0.15625
- lagged: float32 [32, 4, 64, 4096], P('stream', None, None, 'span'), may hold values from -6 to 6
- face_types: int32 [3, 32, 4096], P(None, 'stream', 'span'), may hold values from 0 to 5
- stream_scale: float32 [32, 4096], P('stream', 'span'), may hold values from 1 to 4
- span_scale: float32 [2, 32, 4096], P(None, 'stream', 'span'), may hold values from 0.004 to 0.016
- absorb: float32 [32, 4096], P('stream', 'span'), may hold values from 0.002 to 0.008
- up_blocks: float32 [6, 64, 64], replicated, may hold values from -1 to 0.03
- down_blocks: float32 [6, 64, 64], replicated, may hold values from -1 to 0.03
- diag_inverse: float32 [64, 64], replicated, may hold values from -0.012 to 1
Outputs:
- increment: float32 [32, 4, 64, 4096], P('stream', None, None, 'span')
The draws below stay inside these ranges and needn't reach their ends.
All inputs are finite; a program needn't handle non-finite values.
Results may differ from the reference program's by a relative error of at most 0.00023.
Values sent between devices are 32-bit elements; how exact they have to be, the bound alone decides.
No kernel may reach another device: no remote copies, remote signals or barrier semaphores. Data moves between devices by JAX's collectives and lax.ppermute only.
A program may use at most 64 MiB of HBM per device.

```python
import math
import jax
import jax.numpy as jnp
from jax import lax

P_DOF = 64
TRACERS = 4
NTYPES = 6
NS = 32
NC = 4096


def make_blocks(key, spread, limit):
    key_rates, key_types, key_noise = jax.random.split(key, 3)
    low_loss = jnp.log(0.001)
    high_loss = jnp.log(0.08)
    losses = jnp.exp(jax.random.uniform(key_rates, (P_DOF,), jnp.float32, low_loss, high_loss))
    factors = jax.random.uniform(key_types, (NTYPES, P_DOF), jnp.float32, 0.8, 1.2)
    decays = 1.0 - losses[None, :] * factors
    jitter = jnp.clip(spread * jax.random.normal(key_noise, (NTYPES, P_DOF, P_DOF), jnp.float32), -limit, limit)
    identity = jnp.eye(P_DOF, dtype=jnp.float32)
    return -(decays[:, :, None] * identity) + jitter * (1.0 - identity)


def draw_up_blocks(key, part):
    return make_blocks(jax.random.fold_in(key, 11), 0.01, 0.03)


def draw_down_blocks(key, part):
    return make_blocks(jax.random.fold_in(key, 23), 0.01, 0.03)


def draw_diag_inverse(key, part):
    key_rates, key_noise = jax.random.split(jax.random.fold_in(key, 37))
    losses = jnp.exp(jax.random.uniform(key_rates, (P_DOF,), jnp.float32, jnp.log(0.0005), jnp.log(0.01)))
    jitter = jnp.clip(0.004 * jax.random.normal(key_noise, (P_DOF, P_DOF), jnp.float32), -0.012, 0.012)
    identity = jnp.eye(P_DOF, dtype=jnp.float32)
    return (1.0 - losses)[:, None] * identity + jitter * (1.0 - identity)


def set_ends(values, rng, low, top_value):
    place = [jax.random.randint(jax.random.fold_in(rng, axis), (), 0, length) for axis, length in enumerate(values.shape)]
    longest = values.shape.index(max(values.shape))
    beside = place[:longest] + [(place[longest] + 1) % values.shape[longest]] + place[longest + 1:]
    return values.at[tuple(place)].set(low).at[tuple(beside)].set(top_value)


def shard_levels(own_key, dims, shards, smallest, top_value):
    factor_of, own = 1.0, jax.random.fold_in(own_key, 6)
    for axis_at, parts in shards:
        steps = jnp.exp(jax.random.uniform(jax.random.fold_in(own, axis_at), (parts,), jnp.float32, smallest / len(shards), top_value / len(shards)))
        factor_of = factor_of * jnp.repeat(steps, dims[axis_at] // parts).reshape([-1 if axis == axis_at else 1 for axis in range(len(dims))])
    return factor_of


def scatter_about(key, shape, width, most, cuts=(), held_as=jnp.bfloat16):
    array = jax.random.normal(key, shape, jnp.float32) * width
    if len(cuts) > 0:
        array = shard_levels(key, shape, cuts, -0.22, 0.18) * array
    return jnp.clip(array, min=-most, max=most).astype(held_as)


def setup_inputs(seed: int = 0) -> dict:
    streams_of = jax.random.split(jax.random.key(seed), 10)
    rhs = scatter_about(streams_of[0], (NS, TRACERS, P_DOF, NC), 0.01, 0.15625, ((0, 8), (3, 4)), jnp.float32)
    lagged = scatter_about(streams_of[1], (NS, TRACERS, P_DOF, NC), 1.0, 6.0, ((0, 8), (3, 4)), jnp.float32)
    face_types = set_ends(jax.random.randint(streams_of[2], (3, NS, NC), 0, NTYPES), jax.random.fold_in(streams_of[2], 1), 0, NTYPES - 1).astype(jnp.int32)
    stream_scale = jnp.clip(jnp.exp(math.log(4.0) - 1.3862944 * jax.random.uniform(streams_of[3], (NS, NC), jnp.float32) ** shard_levels(streams_of[3], (NS, NC), ((0, 8), (1, 4)), -0.2, 0.2)), 1.0, 4.0)
    span_scale = jnp.clip(jnp.exp(math.log(0.016) - 1.3862944 * jax.random.uniform(streams_of[4], (2, NS, NC), jnp.float32) ** shard_levels(streams_of[4], (2, NS, NC), ((1, 8), (2, 4)), -0.2, 0.2)), 0.004, 0.016)
    absorb = jnp.clip(jnp.exp(math.log(0.008) - 1.3862944 * jax.random.uniform(streams_of[5], (NS, NC), jnp.float32) ** shard_levels(streams_of[5], (NS, NC), ((0, 8), (1, 4)), -0.2, 0.2)), 0.002, 0.008)
    up_blocks = draw_up_blocks(jax.random.fold_in(streams_of[9], 71), 0)
    down_blocks = draw_down_blocks(jax.random.fold_in(streams_of[9], 71), 0)
    diag_inverse = draw_diag_inverse(jax.random.fold_in(streams_of[9], 71), 0)
    return {"rhs": rhs, "lagged": lagged, "face_types": face_types, "stream_scale": stream_scale, "span_scale": span_scale, "absorb": absorb, "up_blocks": up_blocks, "down_blocks": down_blocks, "diag_inverse": diag_inverse}


precise = lax.Precision.HIGHEST


def typed_apply(blocks_table, type_ids, state_in):
    matrices = blocks_table[type_ids]
    return jnp.einsum('cpq,rqc->rpc', matrices, state_in, precision=precise)


def inverse_apply(diag_inverse, balance, denom_row):
    return jnp.einsum('pq,rqc->rpc', diag_inverse, balance, precision=precise) / denom_row


def reference(rhs, lagged, face_types, stream_scale, span_scale, absorb, up_blocks, down_blocks, diag_inverse):
    denominator = stream_scale + span_scale[0] + span_scale[1] + absorb
    zero_column = jnp.zeros_like(lagged[..., :1])
    lower_side = jnp.concatenate([zero_column, lagged[..., :-1]], axis=3)
    upper_side = jnp.concatenate([lagged[..., 1:], zero_column], axis=3)

    def span_row(pieces):
        low_state, high_state, low_type, high_type, low_scale, high_scale = pieces
        return low_scale * typed_apply(up_blocks, low_type, low_state) + high_scale * typed_apply(up_blocks, high_type, high_state)

    span_terms = lax.map(span_row, (lower_side, upper_side, face_types[1], face_types[2], span_scale[0], span_scale[1]))

    def forward_row(previous, pieces):
        rhs_row, span_here, type_row, scale_row, denom_row = pieces
        balance = rhs_row - span_here - scale_row * typed_apply(up_blocks, type_row, previous)
        solved = inverse_apply(diag_inverse, balance, denom_row)
        return solved, solved

    start_state = jnp.zeros_like(rhs[0])
    unused, forward_part = lax.scan(forward_row, start_state, (rhs, span_terms, face_types[0], stream_scale, denominator))

    def backward_row(carried, pieces):
        part_row, type_row, scale_row, denom_row = pieces
        result = part_row - inverse_apply(diag_inverse, carried, denom_row)
        return scale_row * typed_apply(down_blocks, type_row, result), result

    unused_two, increment = lax.scan(backward_row, start_state, (forward_part, face_types[0], stream_scale, denominator), reverse=True)
    return increment
```

```python
import functools

import jax
import jax.numpy as jnp
from jax import lax
from jax.experimental import pallas as pl
from jax.experimental.pallas import tpu as pltpu
from jax.sharding import PartitionSpec as P

KINDS = 6
MEMBERS = 4
F32 = jnp.float32
BF16 = jnp.bfloat16
VMEM_BYTES = 52 << 20


def parts_of(value):
    high = value.astype(BF16)
    low = (value - high.astype(F32)).astype(BF16)
    return high, low


def stacked_state(value):
    high, low = parts_of(value)
    return jnp.concatenate([high, low, high, low], axis=0)


def stacked_table(value):
    high, low = parts_of(value)
    return jnp.concatenate([high, high, low, low], axis=1)


def kind_masks(kinds_row, rows):
    wide = jnp.broadcast_to(kinds_row, (rows, kinds_row.shape[1]))
    return [wide == t for t in range(1, KINDS)]


def select(products, masks):
    rows = products.shape[0] // KINDS
    chosen = products[:rows]
    for t in range(1, KINDS):
        chosen = jnp.where(masks[t - 1], products[t * rows : (t + 1) * rows], chosen)
    return chosen


def typed(table, state, masks):
    return select(jnp.dot(table, stacked_state(state), preferred_element_type=F32), masks)


def params(flops, moved):
    return dict(
        compiler_params=pltpu.CompilerParams(vmem_limit_bytes=VMEM_BYTES),
        cost_estimate=pl.CostEstimate(flops=flops, bytes_accessed=moved, transcendentals=0),
    )


def tables_kernel(lagged, up, down, inverse, up_out, down_out, inv_out, first_out, last_out, edges, sems):
    layers, tracers, dofs, columns = lagged.shape
    low = pltpu.make_async_copy(lagged.at[:, :, :, pl.ds(0, 128)], edges.at[0], sems.at[0])
    high = pltpu.make_async_copy(lagged.at[:, :, :, pl.ds(columns - 128, 128)], edges.at[1], sems.at[1])
    low.start()
    high.start()
    dinv = inverse[...]
    for t in range(KINDS):
        for source, target in ((up, up_out), (down, down_out)):
            folded = jnp.dot(dinv, source[t], preferred_element_type=F32, precision=lax.Precision.HIGHEST)
            target[t * dofs : (t + 1) * dofs, :] = stacked_table(folded)
    inv_out[...] = stacked_table(dinv)
    low.wait()
    high.wait()
    lane = lax.broadcasted_iota(jnp.int32, (dofs, 128), 1)
    for side, lane_at, target in ((0, 0, first_out), (1, 127, last_out)):
        packed = jnp.zeros((dofs, 128), F32)
        for layer in range(layers):
            for tracer in range(tracers):
                column = edges[side, layer, tracer][:, lane_at : lane_at + 1]
                packed = jnp.where(lane == layer * tracers + tracer, column, packed)
        target[...] = packed


def local_forward_kernel(
    place, rhs, lagged, kinds, stream, span, absorb, from_low, from_high, table, inv_table,
    g_out, f_out, m0, m1, m2, m3, state,
):
    layer = pl.program_id(0)
    layers = pl.num_programs(0)
    tracers, dofs, columns = state.shape
    row = pl.ds(layer, 1)
    scale = stream[row, :]
    span_low = span[0, row, :]
    span_high = span[1, row, :]
    inv_denom = 1.0 / (scale + span_low + span_high + absorb[row, :])
    padding = jnp.zeros((1, 128), jnp.int32)
    kinds_low = pltpu.roll(jnp.concatenate([kinds[1, row, :], padding], axis=1), columns + 127, 1)
    kinds_high = pltpu.roll(jnp.concatenate([kinds[2, row, :], padding], axis=1), 1, 1)
    masks_low = kind_masks(kinds_low, dofs)
    masks_high = kind_masks(kinds_high, dofs)
    turn = lax.rem(128 - layer * tracers, 128)
    edge_low = pltpu.roll(from_low[...], turn, 1)
    edge_high = pltpu.roll(from_high[...], turn, 1)
    lane = lax.broadcasted_iota(jnp.int32, (dofs, 128), 1)
    for tracer in range(tracers):
        beyond = jnp.where(
            lane == 127, edge_low[:, tracer : tracer + 1], edge_high[:, tracer : tracer + 1]
        )
        wide = jnp.concatenate([lagged[0, tracer], beyond], axis=1)
        products = jnp.dot(table[...], stacked_state(wide), preferred_element_type=F32)
        low_term = pltpu.roll(select(products, masks_low), 1, 1)[:, :columns]
        high_term = pltpu.roll(select(products, masks_high), columns + 127, 1)[:, :columns]
        solved = jnp.dot(inv_table[...], stacked_state(rhs[0, tracer]), preferred_element_type=F32)
        g_out[0, tracer] = inv_denom * (solved - span_low * low_term - span_high * high_term)

    @pl.when(layer == 0)
    def first():
        for tracer in range(tracers):
            state[tracer] = g_out[0, tracer]

    @pl.when(layer > 0)
    def later():
        masks = kind_masks(kinds[0, row, :], dofs)
        factor = scale * inv_denom
        for tracer in range(tracers):
            state[tracer] = g_out[0, tracer] - factor * typed(table[...], state[tracer], masks)

    f_out[0] = state[...]

    @pl.when(layer == layers - 1)
    def send():
        count = stream.shape[0]
        width = columns // MEMBERS
        for k, target in enumerate((m0, m1, m2, m3)):
            own = pl.ds(pl.multiple_of((place[0] ^ k) * width, width), width)
            for tracer in range(tracers):
                target[tracer * dofs : (tracer + 1) * dofs, :] = state[tracer, :, own]
            top = tracers * dofs
            scales = stream[:, own]
            target[top : top + count, :] = scales
            target[top + count : top + 2 * count, :] = 1.0 / (
                scales + span[0, :, own] + span[1, :, own] + absorb[:, own]
            )
            target[top + 2 * count : top + 3 * count, :] = kinds[0, :, own].astype(F32)
            if target.shape[0] > top + 3 * count:
                target[top + 3 * count :, :] = jnp.zeros((target.shape[0] - top - 3 * count, width), F32)


def local_backward_kernel(
    place, f_in, kinds, stream, span, absorb, table, m0, m1, m2, m3, carried
):
    step = pl.program_id(0)
    layers = pl.num_programs(0)
    layer = layers - 1 - step
    tracers, dofs, columns = carried.shape
    row = pl.ds(layer, 1)
    scale = stream[row, :]
    inv_denom = 1.0 / (scale + span[0, row, :] + span[1, row, :] + absorb[row, :])
    masks = kind_masks(kinds[0, row, :], dofs)

    @pl.when(step == 0)
    def first():
        for tracer in range(tracers):
            carried[tracer] = scale * typed(table[...], f_in[0, tracer], masks)

    @pl.when(step > 0)
    def later():
        for tracer in range(tracers):
            solved = f_in[0, tracer] - inv_denom * carried[tracer]
            carried[tracer] = scale * typed(table[...], solved, masks)

    @pl.when(step == layers - 1)
    def send():
        width = columns // MEMBERS
        for k, target in enumerate((m0, m1, m2, m3)):
            own = pl.ds(pl.multiple_of((place[0] ^ k) * width, width), width)
            for tracer in range(tracers):
                target[tracer * dofs : (tracer + 1) * dofs, :] = carried[tracer, :, own]


def chain_forward_kernel(
    turn, layers, tracers,
    place, inflow, table, m0, m1, m2, m3, *rest,
):
    olds, (states, out0, out1, out2, out3, outflow, blocks, entering, held, sems, out_sems) = rest[:-11], rest[-11:]
    rows = entering.shape[1]
    dofs = rows // tracers

    @pl.when(place[1] == turn)
    def active():
        arriving = [
            pltpu.make_async_copy(source, blocks.at[place[0] ^ k], sems.at[k])
            for k, source in enumerate((m0, m1, m2, m3))
        ]
        for copy in arriving:
            copy.start()
        if turn == 0:
            entering[0] = jnp.zeros(entering.shape[1:], F32)
        else:
            first = pltpu.make_async_copy(inflow, entering.at[0], sems.at[MEMBERS])
            first.start()
            first.wait()
        for copy in arriving:
            copy.wait()
        for block in range(MEMBERS):
            values = [entering[block, r * dofs : (r + 1) * dofs, :] for r in range(tracers)]
            for layer in range(layers):
                scale = blocks[block, rows + layer : rows + layer + 1, :]
                inv_denom = blocks[block, rows + layers + layer : rows + layers + layer + 1, :]
                kinds = blocks[block, rows + 2 * layers + layer : rows + 2 * layers + layer + 1, :]
                factor = -(scale * inv_denom)
                if block == 0 and turn == 0:
                    values = [jnp.zeros_like(v) for v in values]
                else:
                    masks = kind_masks(kinds, dofs)
                    values = [factor * typed(table[...], v, masks) for v in values]
                for r in range(tracers):
                    held[block, layer, r * dofs : (r + 1) * dofs, :] = values[r]
            pltpu.make_async_copy(held.at[block], states.at[block], out_sems.at[block]).start()
            for r in range(tracers):
                here = slice(r * dofs, (r + 1) * dofs)
                value = values[r] + blocks[block, here, :]
                if block < MEMBERS - 1:
                    entering[block + 1, here, :] = value
                else:
                    outflow[here, :] = value
        leaving = [
            pltpu.make_async_copy(entering.at[place[0] ^ k], target, sems.at[k])
            for k, target in enumerate((out0, out1, out2, out3))
        ]
        for copy in leaving:
            copy.start()
        for copy in leaving:
            copy.wait()
        for block in range(MEMBERS):
            pltpu.make_async_copy(held.at[block], states.at[block], out_sems.at[block]).wait()


def chain_backward_kernel(
    turn, last, layers, tracers,
    place, inflow, table, m0, m1, m2, m3, e0, e1, e2, e3, states, *rest,
):
    olds, (out0, out1, out2, out3, outflow, blocks, terms, entering, held, sems, held_sems) = rest[:-11], rest[-11:]
    rows = entering.shape[1]
    dofs = rows // tracers

    @pl.when(place[1] == turn)
    def active():
        reading = [
            pltpu.make_async_copy(states.at[block], held.at[block], held_sems.at[block])
            for block in range(MEMBERS)
        ]
        for copy in reversed(reading):
            copy.start()
        arriving = [
            pltpu.make_async_copy(source.at[pl.ds(rows, source.shape[0] - rows), :], blocks.at[place[0] ^ k], sems.at[k])
            for k, source in enumerate((m0, m1, m2, m3))
        ] + [
            pltpu.make_async_copy(source, terms.at[place[0] ^ k], sems.at[MEMBERS + k])
            for k, source in enumerate((e0, e1, e2, e3))
        ]
        for copy in arriving:
            copy.start()
        if turn == last:
            entering[MEMBERS - 1] = jnp.zeros(entering.shape[1:], F32)
        else:
            first = pltpu.make_async_copy(inflow, entering.at[MEMBERS - 1], sems.at[2 * MEMBERS])
            first.start()
            first.wait()
        for copy in arriving:
            copy.wait()
        for block in reversed(range(MEMBERS)):
            reading[block].wait()
            if block == 0 and turn == 0:
                continue
            values = [entering[block, r * dofs : (r + 1) * dofs, :] for r in range(tracers)]
            for layer in reversed(range(layers)):
                scale = blocks[block, layer : layer + 1, :]
                inv_denom = blocks[block, layers + layer : layers + layer + 1, :]
                masks = kind_masks(blocks[block, 2 * layers + layer : 2 * layers + layer + 1, :], dofs)
                values = [
                    scale * typed(
                        table[...],
                        held[block, layer, r * dofs : (r + 1) * dofs, :] - inv_denom * values[r],
                        masks,
                    )
                    for r in range(tracers)
                ]
            for r in range(tracers):
                here = slice(r * dofs, (r + 1) * dofs)
                value = values[r] + terms[block, here, :]
                if block > 0:
                    entering[block - 1, here, :] = value
                else:
                    outflow[here, :] = value
        leaving = [
            pltpu.make_async_copy(entering.at[place[0] ^ k], target, sems.at[k])
            for k, target in enumerate((out0, out1, out2, out3))
        ]
        for copy in leaving:
            copy.start()
        for copy in leaving:
            copy.wait()


def take_inflow(place, sources, state):
    tracers, dofs, columns = state.shape
    width = columns // MEMBERS
    for k, source in enumerate(sources):
        own = pl.ds(pl.multiple_of((place[0] ^ k) * width, width), width)
        for tracer in range(tracers):
            state[tracer, :, own] = source[tracer * dofs : (tracer + 1) * dofs, :]


def final_forward_kernel(place, g_in, kinds, stream, span, absorb, table, m0, m1, m2, m3, f_out, state):
    layer = pl.program_id(0)
    tracers, dofs, columns = state.shape
    row = pl.ds(layer, 1)

    @pl.when(layer == 0)
    def first():
        take_inflow(place, (m0, m1, m2, m3), state)

    scale = stream[row, :]
    factor = scale / (scale + span[0, row, :] + span[1, row, :] + absorb[row, :])
    masks = kind_masks(kinds[0, row, :], dofs)
    for tracer in range(tracers):
        value = g_in[0, tracer] - factor * typed(table[...], state[tracer], masks)
        state[tracer] = value
        f_out[0, tracer] = value


def final_backward_kernel(place, f_in, kinds, stream, span, absorb, table, m0, m1, m2, m3, out, carried):
    step = pl.program_id(0)
    layers = pl.num_programs(0)
    layer = layers - 1 - step
    tracers, dofs, columns = carried.shape
    row = pl.ds(layer, 1)

    @pl.when(step == 0)
    def first():
        take_inflow(place, (m0, m1, m2, m3), carried)

    scale = stream[row, :]
    inv_denom = 1.0 / (scale + span[0, row, :] + span[1, row, :] + absorb[row, :])
    for tracer in range(tracers):
        out[0, tracer] = f_in[0, tracer] - inv_denom * carried[tracer]

    @pl.when(step < layers - 1)
    def carry():
        masks = kind_masks(kinds[0, row, :], dofs)
        for tracer in range(tracers):
            carried[tracer] = scale * typed(table[...], out[0, tracer], masks)


def whole(shape, dims):
    return pl.BlockSpec(shape, lambda *i: (0,) * dims)


def per_device(rhs, lagged, kinds, stream, span, absorb, up, down, inverse):
    layers, tracers, dofs, columns = rhs.shape
    rows = tracers * dofs
    width = columns // MEMBERS
    count = lax.axis_size("stream")
    groups = count // MEMBERS
    position = lax.axis_index("stream")
    place = jnp.stack([position % MEMBERS, position // MEMBERS]).astype(jnp.int32)
    long_rows = rows + -(-3 * layers // 8) * 8
    vmem, anywhere, smem = (pl.BlockSpec(memory_space=s) for s in (pltpu.VMEM, pl.ANY, pltpu.SMEM))
    full = functools.partial(jax.ShapeDtypeStruct, dtype=F32)

    up_table, down_table, inv_table, first_edge, last_edge = pl.pallas_call(
        tables_kernel,
        out_shape=(
            jax.ShapeDtypeStruct((KINDS * dofs, 4 * dofs), BF16),
            jax.ShapeDtypeStruct((KINDS * dofs, 4 * dofs), BF16),
            jax.ShapeDtypeStruct((dofs, 4 * dofs), BF16),
            full((dofs, 128)),
            full((dofs, 128)),
        ),
        in_specs=[anywhere, vmem, vmem, vmem],
        out_specs=(vmem,) * 5,
        scratch_shapes=[
            pltpu.VMEM((2, layers, tracers, dofs, 128), F32),
            pltpu.SemaphoreType.DMA((2,)),
        ],
        name="tables",
        **params(1 << 24, 1 << 20),
    )(lagged, up, down, inverse)

    across = lax.axis_size("span")
    from_low = lax.ppermute(last_edge, "span", [(i, i + 1) for i in range(across - 1)])
    from_high = lax.ppermute(first_edge, "span", [(i + 1, i) for i in range(across - 1)])

    def exchanged(messages):
        return [messages[0]] + [
            lax.ppermute(messages[k], "stream", [(i, i ^ k) for i in range(count)])
            for k in range(1, MEMBERS)
        ]

    layer_block = pl.BlockSpec((1, tracers, dofs, columns), lambda i: (i, 0, 0, 0))
    layer_back = pl.BlockSpec((1, tracers, dofs, columns), lambda i: (layers - 1 - i, 0, 0, 0))
    small = [
        whole((3, layers, columns), 3),
        whole((layers, columns), 2),
        whole((2, layers, columns), 3),
        whole((layers, columns), 2),
    ]
    table_block = whole((KINDS * dofs, 4 * dofs), 2)
    message = whole((rows, width), 2)
    long_message = whole((long_rows, width), 2)
    column_state = pltpu.VMEM((tracers, dofs, columns), F32)
    product = 2 * KINDS * dofs * 4 * dofs * tracers * columns

    g, f_zero, *out_b = pl.pallas_call(
        local_forward_kernel,
        grid=(layers,),
        out_shape=(full(rhs.shape), full(rhs.shape)) + (full((long_rows, width)),) * MEMBERS,
        in_specs=[smem, layer_block, layer_block] + small
        + [whole((dofs, 128), 2)] * 2 + [table_block, whole((dofs, 4 * dofs), 2)],
        out_specs=(layer_block, layer_block) + (long_message,) * MEMBERS,
        scratch_shapes=[column_state],
        name="local_forward",
        **params(2 * layers * product, 16 * rhs.size),
    )(place, rhs, lagged, kinds, stream, span, absorb, from_low, from_high, up_table, inv_table)
    in_b = exchanged(out_b)

    out_e = pl.pallas_call(
        local_backward_kernel,
        grid=(layers,),
        out_shape=(full((rows, width)),) * MEMBERS,
        in_specs=[smem, layer_back] + small + [table_block],
        out_specs=(message,) * MEMBERS,
        scratch_shapes=[column_state],
        name="local_backward",
        **params(layers * product, 4 * rhs.size),
    )(place, f_zero, kinds, stream, span, absorb, down_table)
    in_e = exchanged(out_e)

    def between(values, step):
        pairs = [(step * MEMBERS + i, (step + 1) * MEMBERS + i) for i in range(MEMBERS)]
        return lax.ppermute(values, "stream", pairs + [(b, a) for a, b in pairs])

    state_shape = full((MEMBERS, layers, rows, width))
    block_scratch = [
        pltpu.VMEM((MEMBERS, rows, width), F32),
        pltpu.VMEM((MEMBERS, layers, rows, width), F32),
    ]
    inflow = jnp.zeros((rows, width), F32)
    kept = ()
    for turn in range(groups):
        old_count = len(kept)
        *kept, outflow = pl.pallas_call(
            functools.partial(chain_forward_kernel, turn, layers, tracers),
            out_shape=(state_shape,) + (full((rows, width)),) * (MEMBERS + 1),
            in_specs=[smem, anywhere, vmem] + [anywhere] * (MEMBERS + old_count),
            out_specs=(anywhere,) * (MEMBERS + 1) + (vmem,),
            scratch_shapes=[pltpu.VMEM((MEMBERS, long_rows, width), F32)] + block_scratch
            + [pltpu.SemaphoreType.DMA((MEMBERS + 1,)), pltpu.SemaphoreType.DMA((MEMBERS,))],
            input_output_aliases={3 + MEMBERS + i: i for i in range(old_count)},
            name=f"chain_forward_{turn}",
            **params(layers * product, 8 * rhs.size),
        )(place, inflow, up_table, *in_b, *kept)
        if turn < groups - 1:
            inflow = between(outflow, turn)
    states, *out_f = kept
    in_f = exchanged(out_f)

    kept = ()
    for turn in reversed(range(groups)):
        old_count = len(kept)
        *kept, outflow = pl.pallas_call(
            functools.partial(chain_backward_kernel, turn, groups - 1, layers, tracers),
            out_shape=(full((rows, width)),) * (MEMBERS + 1),
            in_specs=[smem, anywhere, vmem] + [anywhere] * (2 * MEMBERS + 1 + old_count),
            out_specs=(anywhere,) * MEMBERS + (vmem,),
            scratch_shapes=[
                pltpu.VMEM((MEMBERS, long_rows - rows, width), F32),
                pltpu.VMEM((MEMBERS, rows, width), F32),
            ] + block_scratch
            + [pltpu.SemaphoreType.DMA((2 * MEMBERS + 1,)), pltpu.SemaphoreType.DMA((MEMBERS,))],
            input_output_aliases={4 + 2 * MEMBERS + i: i for i in range(old_count)},
            name=f"chain_backward_{turn}",
            **params(layers * product, 8 * rhs.size),
        )(place, inflow, down_table, *in_b, *in_e, states, *kept)
        if turn > 0:
            inflow = between(outflow, turn - 1)
    in_h = exchanged(kept)

    f_part = pl.pallas_call(
        final_forward_kernel,
        grid=(layers,),
        out_shape=full(rhs.shape),
        in_specs=[smem, layer_block] + small + [table_block] + [message] * MEMBERS,
        out_specs=layer_block,
        scratch_shapes=[column_state],
        name="final_forward",
        **params(layers * product, 8 * rhs.size),
    )(place, g, kinds, stream, span, absorb, up_table, *in_f)
    return pl.pallas_call(
        final_backward_kernel,
        grid=(layers,),
        out_shape=full(rhs.shape),
        in_specs=[smem, layer_back] + small + [table_block] + [message] * MEMBERS,
        out_specs=layer_back,
        scratch_shapes=[column_state],
        name="final_backward",
        **params(layers * product, 8 * rhs.size),
    )(place, f_part, kinds, stream, span, absorb, down_table, *in_h)


def solution(mesh):
    return jax.shard_map(
        per_device,
        mesh=mesh,
        in_specs=(
            P("stream", None, None, "span"),
            P("stream", None, None, "span"),
            P(None, "stream", "span"),
            P("stream", "span"),
            P(None, "stream", "span"),
            P("stream", "span"),
            P(),
            P(),
            P(),
        ),
        out_specs=P("stream", None, None, "span"),
        check_vma=False,
    )
```

```python
import functools

import jax
import jax.numpy as jnp
from jax import lax
from jax.experimental import pallas as pl
from jax.experimental.pallas import tpu as pltpu
from jax.sharding import PartitionSpec as P

KINDS = 6
MEMBERS = 4
F32 = jnp.float32
BF16 = jnp.bfloat16


def parts_of(value):
    high = value.astype(BF16)
    low = (value - high.astype(F32)).astype(BF16)
    return high, low


def stacked_state(value):
    high, low = parts_of(value)
    return jnp.concatenate([high, low, high, low], axis=0)


def stacked_table(value):
    high, low = parts_of(value)
    return jnp.concatenate([high, high, low, low], axis=1)


def kind_masks(kinds_row, rows):
    wide = jnp.broadcast_to(kinds_row, (rows, kinds_row.shape[1]))
    return [wide == t for t in range(1, KINDS)]


def select(products, masks):
    rows = products.shape[0] // KINDS
    chosen = products[:rows]
    for t in range(1, KINDS):
        chosen = jnp.where(masks[t - 1], products[t * rows : (t + 1) * rows], chosen)
    return chosen


def typed(table, state, masks):
    return select(jnp.dot(table, stacked_state(state), preferred_element_type=F32), masks)


def params(flops, moved, vmem):
    return dict(
        compiler_params=pltpu.CompilerParams(vmem_limit_bytes=vmem),
        cost_estimate=pl.CostEstimate(flops=flops, bytes_accessed=moved, transcendentals=0),
    )


def edges_kernel(place, lagged, pair_out, cross_out, edges, sems):
    layers, tracers, dofs, columns = lagged.shape
    low = pltpu.make_async_copy(lagged.at[:, :, :, pl.ds(0, 128)], edges.at[0], sems.at[0])
    high = pltpu.make_async_copy(lagged.at[:, :, :, pl.ds(columns - 128, 128)], edges.at[1], sems.at[1])
    low.start()
    high.start()
    low.wait()
    high.wait()
    lane = lax.broadcasted_iota(jnp.int32, (dofs, 128), 1)
    packed = []
    for side, lane_at in ((0, 0), (1, 127)):
        value = jnp.zeros((dofs, 128), F32)
        for layer in range(layers):
            for tracer in range(tracers):
                column = edges[side, layer, tracer][:, lane_at : lane_at + 1]
                value = jnp.where(lane == layer * 2 * tracers + tracer, column, value)
        packed.append(value)
    first, last = packed
    odd = place[2] == 1
    pair_out[...] = jnp.where(odd, first, last)
    cross_out[...] = jnp.where(odd, last, first)


def tables_kernel(up, down, inverse, up_out, down_out, inv_out, ups, downs, inv, sems):
    dofs = inv.shape[0]
    copies = [
        pltpu.make_async_copy(source, target, sems.at[i])
        for i, (source, target) in enumerate(((up, ups), (down, downs), (inverse, inv)))
    ]
    for copy in copies:
        copy.start()
    for copy in copies:
        copy.wait()
    dinv = inv[...]
    for t in range(KINDS):
        for source, target in ((ups, up_out), (downs, down_out)):
            folded = jnp.dot(dinv, source[t], preferred_element_type=F32, precision=lax.Precision.HIGHEST)
            target[t * dofs : (t + 1) * dofs, :] = stacked_table(folded)
    inv_out[...] = stacked_table(dinv)


def local_forward_kernel(
    place, rhs, lagged, kinds, stream, span, absorb, table, inv_table,
    g_out, f_out, m0, m1, m2, m3,
):
    layer = pl.program_id(0)
    layers, tracers, dofs, columns = g_out.shape
    row = pl.ds(layer, 1)
    scale = stream[row, :]
    span_low = span[0, row, :]
    span_high = span[1, row, :]
    inv_denom = 1.0 / (scale + span_low + span_high + absorb[row, :])
    lane = lax.broadcasted_iota(jnp.int32, (1, columns), 1)
    weight_low = jnp.where(lane == 0, 0.0, inv_denom * span_low)
    weight_high = jnp.where(lane == columns - 1, 0.0, inv_denom * span_high)
    masks_low = kind_masks(pltpu.roll(kinds[1, row, :], columns - 1, 1), dofs)
    masks_high = kind_masks(pltpu.roll(kinds[2, row, :], 1, 1), dofs)
    for tracer in range(tracers):
        products = jnp.dot(table[...], stacked_state(lagged[0, tracer]), preferred_element_type=F32)
        low_term = pltpu.roll(select(products, masks_low), 1, 1)
        high_term = pltpu.roll(select(products, masks_high), columns - 1, 1)
        solved = jnp.dot(inv_table[...], stacked_state(rhs[0, tracer]), preferred_element_type=F32)
        g_out[layer, tracer] = inv_denom * solved - weight_low * low_term - weight_high * high_term

    @pl.when(layer == 0)
    def first():
        for tracer in range(tracers):
            f_out[0, tracer] = g_out[0, tracer]

    @pl.when(layer > 0)
    def later():
        masks = kind_masks(kinds[0, row, :], dofs)
        factor = scale * inv_denom
        for tracer in range(tracers):
            f_out[layer, tracer] = g_out[layer, tracer] - factor * typed(
                table[...], f_out[layer - 1, tracer], masks
            )

    @pl.when(layer == layers - 1)
    def send():
        width = columns // MEMBERS
        for k, target in enumerate((m0, m1, m2, m3)):
            own = pl.ds(pl.multiple_of((place[0] ^ k) * width, width), width)
            for tracer in range(tracers):
                target[tracer * dofs : (tracer + 1) * dofs, :] = f_out[layers - 1, tracer, :, own]
            top = tracers * dofs
            scales = stream[:, own]
            target[top : top + layers, :] = scales
            target[top + layers : top + 2 * layers, :] = 1.0 / (
                scales + span[0, :, own] + span[1, :, own] + absorb[:, own]
            )
            target[top + 2 * layers : top + 3 * layers, :] = kinds[0, :, own].astype(F32)
            if target.shape[0] > top + 3 * layers:
                target[top + 3 * layers :, :] = jnp.zeros((target.shape[0] - top - 3 * layers, width), F32)


def edge_fix_kernel(
    place, pair, cross, kinds, stream, span, absorb, table, m0, m1, m2, m3,
    g_fix, f_fix, o0, o1, o2, o3,
):
    layers, columns = stream.shape
    dofs = pair.shape[0]
    width = m0.shape[1]
    tracers = m0.shape[0] // dofs
    both = 2 * tracers
    for source, target in ((m0, o0), (m1, o1), (m2, o2), (m3, o3)):
        target[...] = source[...]
    odd = place[2] == 1
    from_low = jnp.where(odd, pair[...], cross[...])
    from_high = jnp.where(odd, cross[...], pair[...])
    lane = lax.broadcasted_iota(jnp.int32, (1, 128), 1)
    halo = jnp.where(lane % both < tracers, from_low, pltpu.roll(from_high, tracers, 1))
    side_kinds = jnp.zeros((1, 128), jnp.int32)
    own_kinds = jnp.zeros((1, 128), jnp.int32)
    weight = jnp.zeros((1, 128), F32)
    factor = jnp.zeros((1, 128), F32)
    for layer in range(layers):
        row = slice(layer, layer + 1)
        for side, tile, at in ((0, 0, 0), (1, columns - 128, 127)):
            def one(value):
                return value[:, at : at + 1]

            here = lane // tracers == 2 * layer + side
            cut = slice(tile, tile + 128)
            scale = stream[row, cut]
            inv_denom = 1.0 / (scale + span[0, row, cut] + span[1, row, cut] + absorb[row, cut])
            side_kinds = jnp.where(here, one(kinds[1 + side, row, cut]), side_kinds)
            own_kinds = jnp.where(here, one(kinds[0, row, cut]), own_kinds)
            weight = jnp.where(here, one(inv_denom * span[side, row, cut]), weight)
            if layer > 0:
                factor = jnp.where(here, one(inv_denom * scale), factor)
    change = -(weight * typed(table[...], halo, kind_masks(side_kinds, dofs)))
    g_fix[...] = change
    masks = kind_masks(own_kinds, dofs)
    running = change
    for layer in range(1, layers):
        running = change - factor * typed(table[...], pltpu.roll(running, both, 1), masks)
    f_fix[...] = running
    top = (layers - 1) * both
    for k, target in enumerate((o0, o1, o2, o3)):
        @pl.when(place[0] ^ k == 0)
        def low():
            for tracer in range(tracers):
                here = slice(tracer * dofs, (tracer + 1) * dofs)
                column = running[:, top + tracer : top + tracer + 1]
                target[here, 0:128] = target[here, 0:128] + jnp.where(lane == 0, column, 0.0)

        @pl.when(place[0] ^ k == MEMBERS - 1)
        def high():
            for tracer in range(tracers):
                here = slice(tracer * dofs, (tracer + 1) * dofs)
                at = top + tracers + tracer
                column = running[:, at : at + 1]
                target[here, width - 128 : width] = target[here, width - 128 : width] + jnp.where(
                    lane == 127, column, 0.0
                )


def with_edges(value, fix, layer, tracer, tracers):
    columns = value.shape[1]
    lane = lax.broadcasted_iota(jnp.int32, (1, 128), 1)
    at = layer * 2 * tracers + tracer
    low = value[:, :128] + jnp.where(lane == 0, fix[:, at : at + 1], 0.0)
    at = at + tracers
    high = value[:, columns - 128 :] + jnp.where(lane == 127, fix[:, at : at + 1], 0.0)
    return jnp.concatenate([low, value[:, 128 : columns - 128], high], axis=1)


def local_backward_kernel(
    place, f_in, f_fix, kinds, stream, span, absorb, table, m0, m1, m2, m3, carried
):
    layers, tracers, dofs, columns = f_in.shape
    for layer in reversed(range(layers)):
        row = slice(layer, layer + 1)
        scale = stream[row, :]
        inv_denom = 1.0 / (scale + span[0, row, :] + span[1, row, :] + absorb[row, :])
        masks = kind_masks(kinds[0, row, :], dofs)
        for tracer in range(tracers):
            solved = with_edges(f_in[layer, tracer], f_fix[...], layer, tracer, tracers)
            if layer < layers - 1:
                solved = solved - inv_denom * carried[tracer]
            carried[tracer] = scale * typed(table[...], solved, masks)
    width = columns // MEMBERS
    for k, target in enumerate((m0, m1, m2, m3)):
        own = pl.ds(pl.multiple_of((place[0] ^ k) * width, width), width)
        for tracer in range(tracers):
            target[tracer * dofs : (tracer + 1) * dofs, :] = carried[tracer, :, own]


def chain_rows(block_ref, top, layers, layer):
    def row(which):
        at = top + which * layers + layer
        return block_ref[at : at + 1, :]

    return row(0), row(1), row(2)


def forward_chain(turn, layers, tracers, table, blocks, entering, held, outflow):
    rows = entering.shape[1]
    dofs = rows // tracers
    for block in range(MEMBERS):
        idle = block == 0 and turn == 0
        values = [entering[block, r * dofs : (r + 1) * dofs, :] for r in range(tracers)]
        for layer in range(layers):
            if not idle:
                scale, inv_denom, kinds = chain_rows(blocks.at[block], rows, layers, layer)
                masks = kind_masks(kinds, dofs)
                factor = -(scale * inv_denom)
                values = [factor * typed(table[...], v, masks) for v in values]
            for r in range(tracers):
                held[block, layer, r * dofs : (r + 1) * dofs, :] = values[r]
        for r in range(tracers):
            here = slice(r * dofs, (r + 1) * dofs)
            value = values[r] + blocks[block, here, :]
            if block < MEMBERS - 1:
                entering[block + 1, here, :] = value
            elif outflow is not None:
                outflow[here, :] = value


def backward_chain(turn, layers, tracers, table, blocks, terms, entering, held, outflow):
    rows = entering.shape[1]
    dofs = rows // tracers
    for block in reversed(range(MEMBERS)):
        if block == 0 and turn == 0:
            continue
        values = [entering[block, r * dofs : (r + 1) * dofs, :] for r in range(tracers)]
        for layer in reversed(range(layers)):
            scale, inv_denom, kinds = chain_rows(blocks.at[block], rows, layers, layer)
            masks = kind_masks(kinds, dofs)
            values = [
                scale * typed(
                    table[...],
                    held[block, layer, r * dofs : (r + 1) * dofs, :] - inv_denom * values[r],
                    masks,
                )
                for r in range(tracers)
            ]
        for r in range(tracers):
            here = slice(r * dofs, (r + 1) * dofs)
            value = values[r] + terms[block, here, :]
            if block > 0:
                entering[block - 1, here, :] = value
            else:
                outflow[here, :] = value


def take(place, sources, target):
    for k, source in enumerate(sources):
        target[place[0] ^ k] = source[...]


def give(place, targets, source):
    for k, target in enumerate(targets):
        target[...] = source[place[0] ^ k]


def keep(place, turn, olds, targets):
    if olds:
        @pl.when(place[1] != turn)
        def passed():
            for old, target in zip(olds, targets):
                target[...] = old[...]


def chain_forward_kernel(turn, layers, tracers, place, inflow, table, m0, m1, m2, m3, *rest):
    olds, (states, o0, o1, o2, o3, outflow, blocks, entering) = rest[:-8], rest[-8:]
    outs = (o0, o1, o2, o3)

    @pl.when(place[1] == turn)
    def active():
        take(place, (m0, m1, m2, m3), blocks)
        entering[0] = inflow[...] if turn > 0 else jnp.zeros(inflow.shape, F32)
        forward_chain(turn, layers, tracers, table, blocks, entering, states, outflow)
        give(place, outs, entering)

    keep(place, turn, olds, outs)


def chain_last_kernel(
    turn, layers, tracers, place, inflow, up_table, down_table, m0, m1, m2, m3, e0, e1, e2, e3, *rest
):
    olds, (o0, o1, o2, o3, h0, h1, h2, h3, outflow, blocks, terms, entering, returning, held) = rest[:-14], rest[-14:]
    outs = (o0, o1, o2, o3)

    @pl.when(place[1] == turn)
    def active():
        take(place, (m0, m1, m2, m3), blocks)
        take(place, (e0, e1, e2, e3), terms)
        entering[0] = inflow[...] if turn > 0 else jnp.zeros(inflow.shape, F32)
        forward_chain(turn, layers, tracers, up_table, blocks, entering, held, None)
        returning[MEMBERS - 1] = jnp.zeros(inflow.shape, F32)
        backward_chain(turn, layers, tracers, down_table, blocks, terms, returning, held, outflow)
        give(place, outs, entering)
        give(place, (h0, h1, h2, h3), returning)

    keep(place, turn, olds, outs)


def chain_backward_kernel(
    turn, layers, tracers, place, inflow, table, m0, m1, m2, m3, e0, e1, e2, e3, states, *rest
):
    olds, (o0, o1, o2, o3, outflow, blocks, terms, returning) = rest[:-8], rest[-8:]
    outs = (o0, o1, o2, o3)

    @pl.when(place[1] == turn)
    def active():
        take(place, (m0, m1, m2, m3), blocks)
        take(place, (e0, e1, e2, e3), terms)
        returning[MEMBERS - 1] = inflow[...]
        backward_chain(turn, layers, tracers, table, blocks, terms, returning, states, outflow)
        give(place, outs, returning)

    keep(place, turn, olds, outs)


def take_inflow(place, sources, state):
    tracers, dofs, columns = state.shape
    width = columns // MEMBERS
    for k, source in enumerate(sources):
        own = pl.ds(pl.multiple_of((place[0] ^ k) * width, width), width)
        for tracer in range(tracers):
            state[tracer, :, own] = source[tracer * dofs : (tracer + 1) * dofs, :]


def final_forward_kernel(
    place, g_in, g_fix, kinds, stream, span, absorb, table, m0, m1, m2, m3, f_out, state
):
    layers, tracers, dofs, columns = g_in.shape
    take_inflow(place, (m0, m1, m2, m3), state)
    for layer in range(layers):
        row = slice(layer, layer + 1)
        scale = stream[row, :]
        factor = scale / (scale + span[0, row, :] + span[1, row, :] + absorb[row, :])
        masks = kind_masks(kinds[0, row, :], dofs)
        for tracer in range(tracers):
            before = state[tracer] if layer == 0 else f_out[layer - 1, tracer]
            here = with_edges(g_in[layer, tracer], g_fix[...], layer, tracer, tracers)
            f_out[layer, tracer] = here - factor * typed(table[...], before, masks)


def final_backward_kernel(
    place, f_in, kinds, stream, span, absorb, table, m0, m1, m2, m3, out, carried, solved, sems
):
    layers, tracers, dofs, columns = f_in.shape
    take_inflow(place, (m0, m1, m2, m3), carried)
    copies = []
    for layer in reversed(range(layers)):
        row = slice(layer, layer + 1)
        scale = stream[row, :]
        inv_denom = 1.0 / (scale + span[0, row, :] + span[1, row, :] + absorb[row, :])
        for tracer in range(tracers):
            solved[layer, tracer] = f_in[layer, tracer] - inv_denom * carried[tracer]
            if layer == 0:
                copies.append(pltpu.make_async_copy(solved.at[0, tracer], out.at[0, tracer], sems.at[layers + tracer]))
                copies[-1].start()
        if layer > 0:
            copies.append(pltpu.make_async_copy(solved.at[layer], out.at[layer], sems.at[layer]))
            copies[-1].start()
            masks = kind_masks(kinds[0, row, :], dofs)
            for tracer in range(tracers):
                carried[tracer] = scale * typed(table[...], solved[layer, tracer], masks)
    for copy in copies:
        copy.wait()


def whole(shape, dims):
    return pl.BlockSpec(shape, lambda *i: (0,) * dims)


def per_device(rhs, lagged, kinds, stream, span, absorb, up, down, inverse):
    layers, tracers, dofs, columns = rhs.shape
    rows = tracers * dofs
    width = columns // MEMBERS
    count = lax.axis_size("stream")
    groups = count // MEMBERS
    position = lax.axis_index("stream")
    place = jnp.stack(
        [position % MEMBERS, position // MEMBERS, lax.axis_index("span") % 2]
    ).astype(jnp.int32)
    long_rows = rows + -(-3 * layers // 8) * 8
    vmem, anywhere, smem = (pl.BlockSpec(memory_space=s) for s in (pltpu.VMEM, pl.ANY, pltpu.SMEM))
    full = functools.partial(jax.ShapeDtypeStruct, dtype=F32)
    field = 4 * rhs.size
    product = 2 * KINDS * dofs * 4 * dofs * tracers * columns
    some = 12 << 20
    table_shape = (KINDS * dofs, 4 * dofs)

    pair_edge, cross_edge = pl.pallas_call(
        edges_kernel,
        out_shape=(full((dofs, 128)),) * 2,
        in_specs=[smem, anywhere],
        out_specs=(vmem,) * 2,
        scratch_shapes=[
            pltpu.VMEM((2, layers, tracers, dofs, 128), F32),
            pltpu.SemaphoreType.DMA((2,)),
        ],
        name="edges",
        **params(1 << 20, 1 << 20, some),
    )(place, lagged)
    across = lax.axis_size("span")
    crossing = [(i, i + 1) for i in range(1, across - 1, 2)]
    pair = lax.ppermute(pair_edge, "span", [(i, i ^ 1) for i in range(across)])
    cross = lax.ppermute(cross_edge, "span", crossing + [(b, a) for a, b in crossing])

    up_table, down_table, inv_table = pl.pallas_call(
        tables_kernel,
        out_shape=(
            jax.ShapeDtypeStruct(table_shape, BF16),
            jax.ShapeDtypeStruct(table_shape, BF16),
            jax.ShapeDtypeStruct((dofs, 4 * dofs), BF16),
        ),
        in_specs=[anywhere] * 3,
        out_specs=(vmem,) * 3,
        scratch_shapes=[
            pltpu.VMEM(up.shape, F32),
            pltpu.VMEM(down.shape, F32),
            pltpu.VMEM(inverse.shape, F32),
            pltpu.SemaphoreType.DMA((3,)),
        ],
        name="tables",
        **params(1 << 24, 1 << 20, some),
    )(up, down, inverse)

    def exchanged(messages):
        return [messages[0]] + [
            lax.ppermute(messages[k], "stream", [(i, i ^ k) for i in range(count)])
            for k in range(1, MEMBERS)
        ]

    def between(values, step):
        pairs = [(step * MEMBERS + i, (step + 1) * MEMBERS + i) for i in range(MEMBERS)]
        return lax.ppermute(values, "stream", pairs + [(b, a) for a, b in pairs])

    layer_block = pl.BlockSpec((1, tracers, dofs, columns), lambda i: (i, 0, 0, 0))
    small = (kinds, stream, span, absorb)
    small_blocks = [
        whole((3, layers, columns), 3),
        whole((layers, columns), 2),
        whole((2, layers, columns), 3),
        whole((layers, columns), 2),
    ]
    column_state = pltpu.VMEM((tracers, dofs, columns), F32)
    message = full((rows, width))
    long_message = full((long_rows, width))
    fix = full((dofs, 128))

    g, f_zero, *out_b = pl.pallas_call(
        local_forward_kernel,
        grid=(layers,),
        out_shape=(full(rhs.shape), full(rhs.shape)) + (long_message,) * MEMBERS,
        in_specs=[smem, layer_block, layer_block] + small_blocks
        + [whole(table_shape, 2), whole((dofs, 4 * dofs), 2)],
        out_specs=(whole(rhs.shape, 4),) * 2 + (whole((long_rows, width), 2),) * MEMBERS,
        name="local_forward",
        **params(3 * layers * product, 8 * rhs.size, some + 2 * field + (16 << 20)),
    )(place, rhs, lagged, *small, up_table, inv_table)

    g_fix, f_fix, *out_b = pl.pallas_call(
        edge_fix_kernel,
        out_shape=(fix, fix) + (long_message,) * MEMBERS,
        in_specs=[smem] + [vmem] * (7 + MEMBERS),
        out_specs=(vmem,) * (2 + MEMBERS),
        name="edge_fix",
        **params(1 << 24, 1 << 20, some),
    )(place, pair, cross, *small, up_table, *out_b)
    in_b = exchanged(out_b)

    out_e = pl.pallas_call(
        local_backward_kernel,
        out_shape=(message,) * MEMBERS,
        in_specs=[smem] + [vmem] * 7,
        out_specs=(vmem,) * MEMBERS,
        scratch_shapes=[column_state],
        name="local_backward",
        **params(layers * product, 4 * rhs.size, some + field),
    )(place, f_zero, f_fix, *small, down_table)
    in_e = exchanged(out_e)
    in_b, _ = lax.optimization_barrier((in_b, out_e))

    blocks = pltpu.VMEM((MEMBERS, long_rows, width), F32)
    inner = pltpu.VMEM((MEMBERS, rows, width), F32)
    held = (MEMBERS, layers, rows, width)
    inflow = jnp.zeros((rows, width), F32)
    states, out_f = [], []
    for turn in range(groups - 1):
        state, *out_f, outflow = pl.pallas_call(
            functools.partial(chain_forward_kernel, turn, layers, tracers),
            out_shape=(full(held),) + (message,) * (MEMBERS + 1),
            in_specs=[smem] + [vmem] * (2 + MEMBERS + len(out_f)),
            out_specs=(vmem,) * (MEMBERS + 2),
            scratch_shapes=[blocks, inner],
            name=f"chain_forward_{turn}",
            **params(layers * product, 8 * rhs.size, some + field),
        )(place, inflow, up_table, *in_b, *out_f)
        states.append(state)
        inflow = between(outflow, turn)

    *out_f, h0, h1, h2, h3, outflow = pl.pallas_call(
        functools.partial(chain_last_kernel, groups - 1, layers, tracers),
        out_shape=(message,) * (2 * MEMBERS + 1),
        in_specs=[smem] + [vmem] * (3 + 2 * MEMBERS + len(out_f)),
        out_specs=(vmem,) * (2 * MEMBERS + 1),
        scratch_shapes=[blocks, inner, inner, inner, pltpu.VMEM(held, F32)],
        name="chain_last",
        **params(2 * layers * product, 8 * rhs.size, some + 2 * field),
    )(place, inflow, up_table, down_table, *in_b, *in_e, *out_f)
    in_f = exchanged(out_f)

    out_h = [h0, h1, h2, h3]
    for turn in reversed(range(groups - 1)):
        inflow = between(outflow, turn)
        *out_h, outflow = pl.pallas_call(
            functools.partial(chain_backward_kernel, turn, layers, tracers),
            out_shape=(message,) * (MEMBERS + 1),
            in_specs=[smem] + [vmem] * (3 + 3 * MEMBERS),
            out_specs=(vmem,) * (MEMBERS + 1),
            scratch_shapes=[blocks, inner, inner],
            name=f"chain_backward_{turn}",
            **params(layers * product, 8 * rhs.size, some + field),
        )(place, inflow, down_table, *in_b, *in_e, states[turn], *out_h)
    in_h = exchanged(out_h)

    f_part = pl.pallas_call(
        final_forward_kernel,
        out_shape=full(rhs.shape),
        in_specs=[smem] + [vmem] * (7 + MEMBERS),
        out_specs=vmem,
        scratch_shapes=[column_state],
        name="final_forward",
        **params(layers * product, 8 * rhs.size, some + 2 * field),
    )(place, g, g_fix, *small, up_table, *in_f)
    return pl.pallas_call(
        final_backward_kernel,
        out_shape=full(rhs.shape),
        in_specs=[smem] + [vmem] * (6 + MEMBERS),
        out_specs=anywhere,
        scratch_shapes=[
            column_state,
            pltpu.VMEM(rhs.shape, F32),
            pltpu.SemaphoreType.DMA((layers + tracers,)),
        ],
        name="final_backward",
        **params(layers * product, 8 * rhs.size, some + 2 * field),
    )(place, f_part, *small, down_table, *in_h)


def solution(mesh):
    return jax.shard_map(
        per_device,
        mesh=mesh,
        in_specs=(
            P("stream", None, None, "span"),
            P("stream", None, None, "span"),
            P(None, "stream", "span"),
            P("stream", "span"),
            P(None, "stream", "span"),
            P("stream", "span"),
            P(),
            P(),
            P(),
        ),
        out_specs=P("stream", None, None, "span"),
        check_vma=False,
    )
```

```python
import functools

import jax
import jax.numpy as jnp
from jax import lax
from jax.experimental import pallas as pl
from jax.experimental.pallas import tpu as pltpu
from jax.sharding import PartitionSpec as P

KINDS = 6
MEMBERS = 4
PIECE = 256
F32 = jnp.float32
BF16 = jnp.bfloat16


def parts_of(value):
    high = value.astype(BF16)
    low = (value - high.astype(F32)).astype(BF16)
    return high, low


def stacked_state(value):
    high, low = parts_of(value)
    return jnp.concatenate([high, low, high, low], axis=0)


def stacked_table(value):
    high, low = parts_of(value)
    return jnp.concatenate([high, high, low, low], axis=1)


def kind_masks(kinds_row, rows):
    wide = jnp.broadcast_to(kinds_row, (rows, kinds_row.shape[1]))
    return [wide == t for t in range(1, KINDS)]


def select(products, masks):
    rows = products.shape[0] // KINDS
    chosen = products[:rows]
    for t in range(1, KINDS):
        chosen = jnp.where(masks[t - 1], products[t * rows : (t + 1) * rows], chosen)
    return chosen


def typed(table, state, masks):
    return select(jnp.dot(table, stacked_state(state), preferred_element_type=F32), masks)


def params(flops, moved, vmem):
    return dict(
        compiler_params=pltpu.CompilerParams(vmem_limit_bytes=vmem),
        cost_estimate=pl.CostEstimate(flops=flops, bytes_accessed=moved, transcendentals=0),
    )


def pieces(columns):
    return [slice(at, at + PIECE) for at in range(0, columns, PIECE)]


def span_kernel(
    rhs, lagged, kinds, stream, span, absorb, up, down, inverse,
    g_hbm, meta, sides, edges, up_table, down_table,
    inv_table, g_out, rhs_in, lagged_in, kinds_in, stream_in, span_in, absorb_in, ups, downs, inv, sems, out_sems,
):
    layers, tracers, dofs, columns = g_out.shape
    small = [
        pltpu.make_async_copy(source, target, sems.at[2 * layers + i])
        for i, (source, target) in enumerate(
            (
                (up, ups), (inverse, inv), (down, downs),
                (kinds, kinds_in), (stream, stream_in), (span, span_in), (absorb, absorb_in),
            )
        )
    ]

    def loads(layer):
        return (
            pltpu.make_async_copy(lagged.at[layer], lagged_in.at[layer], sems.at[2 * layer]),
            pltpu.make_async_copy(rhs.at[layer], rhs_in.at[layer], sems.at[2 * layer + 1]),
        )

    def store(layer):
        return pltpu.make_async_copy(g_out.at[layer], g_hbm.at[layer], out_sems.at[layer])

    for copy in small:
        copy.start()
    for layer in range(layers):
        for copy in loads(layer):
            copy.start()
    for copy in small:
        copy.wait()
    dinv = inv[...]
    for t in range(KINDS):
        for source, target in ((ups, up_table), (downs, down_table)):
            folded = jnp.dot(dinv, source[t], preferred_element_type=F32, precision=lax.Precision.HIGHEST)
            target[t * dofs : (t + 1) * dofs, :] = stacked_table(folded)
    inv_table[...] = stacked_table(dinv)
    scales = stream_in[...]
    inv_denoms = 1.0 / (scales + span_in[0] + span_in[1] + absorb_in[...])
    for i, rows in enumerate((scales, inv_denoms, scales * inv_denoms, kinds_in[0].astype(F32))):
        meta[i * layers : (i + 1) * layers, :] = rows
    lane = lax.broadcasted_iota(jnp.int32, (1, 128), 1)
    wide_lane = lax.broadcasted_iota(jnp.int32, (1, columns), 1)
    sides[...] = jnp.zeros(sides.shape, F32)
    edges[...] = jnp.zeros(edges.shape, F32)

    def step(layer, carry):
        row = pl.ds(layer, 1)
        inv_denom = meta[pl.ds(layers + layer, 1), :]
        weight_low = inv_denom * span_in[0, row, :]
        weight_high = inv_denom * span_in[1, row, :]
        kinds_low = kinds_in[1, row, :]
        kinds_high = kinds_in[2, row, :]
        for side, weight, kind, at in (
            (0, weight_low, kinds_low, 0),
            (1, weight_high, kinds_high, columns - 1),
        ):
            here = lane // tracers == 2 * layer + side
            sides[0:1, :] = jnp.where(here, kind[:, at : at + 1].astype(F32), sides[0:1, :])
            sides[1:2, :] = jnp.where(here, weight[:, at : at + 1], sides[1:2, :])
        weight_low = jnp.where(wide_lane == 0, 0.0, weight_low)
        weight_high = jnp.where(wide_lane == columns - 1, 0.0, weight_high)
        kinds_low = pltpu.roll(kinds_low, columns - 1, 1)
        kinds_high = pltpu.roll(kinds_high, 1, 1)
        for copy in loads(layer):
            copy.wait()
        edge_values = edges[...]
        for tracer in range(tracers):
            for side, at in ((0, 0), (1, columns - 1)):
                here = lane == side * 64 + layer * 2 * tracers + tracer
                edge_values = jnp.where(here, lagged_in[layer, tracer, :, at : at + 1], edge_values)
        edges[...] = edge_values
        for tracer in range(tracers):
            lows, highs, solved = [], [], []
            for piece in pieces(columns):
                products = jnp.dot(
                    up_table[...], stacked_state(lagged_in[layer, tracer, :, piece]), preferred_element_type=F32
                )
                lows.append(select(products, kind_masks(kinds_low[:, piece], dofs)))
                highs.append(select(products, kind_masks(kinds_high[:, piece], dofs)))
                solved.append(
                    jnp.dot(
                        inv_table[...], stacked_state(rhs_in[layer, tracer, :, piece]), preferred_element_type=F32
                    )
                )
            low_term = pltpu.roll(jnp.concatenate(lows, axis=1), 1, 1)
            high_term = pltpu.roll(jnp.concatenate(highs, axis=1), columns - 1, 1)
            g_out[layer, tracer] = (
                inv_denom * jnp.concatenate(solved, axis=1) - weight_low * low_term - weight_high * high_term
            )
        store(layer).start()
        return carry

    lax.fori_loop(0, layers, step, 0)
    for layer in range(layers):
        store(layer).wait()


def edge_value(fix, layer, tracer, tracers, side):
    lane = lax.broadcasted_iota(jnp.int32, (1, 128), 1)
    at = (2 * layer + side) * tracers + tracer
    return jnp.where(lane == (127 if side else 0), fix[:, at : at + 1], 0.0)


def with_edges(value, fix, layer, tracer, tracers, piece, columns):
    if piece.start == 0:
        low = value[:, :128] + edge_value(fix, layer, tracer, tracers, 0)
        value = jnp.concatenate([low, value[:, 128:]], axis=1)
    if piece.stop == columns:
        end = value.shape[1] - 128
        high = value[:, end:] + edge_value(fix, layer, tracer, tracers, 1)
        value = jnp.concatenate([value[:, :end], high], axis=1)
    return value


def local_forward_kernel(
    place, pair, cross, g_hbm, meta, sides, table, f_out, m0, m1, m2, m3, g_in, sems
):
    layers, tracers, dofs, columns = g_in.shape
    copies = [pltpu.make_async_copy(g_hbm.at[layer], g_in.at[layer], sems.at[layer]) for layer in range(layers)]
    for copy in copies:
        copy.start()
    odd = place[2] == 1
    from_low = pltpu.roll(jnp.where(odd, pair[...], cross[...]), 64, 1)
    from_high = pltpu.roll(jnp.where(odd, cross[...], pair[...]), tracers, 1)
    lane = lax.broadcasted_iota(jnp.int32, (1, 128), 1)
    halo = jnp.where(lane % (2 * tracers) < tracers, from_low, from_high)
    fix = -(sides[1:2, :] * typed(table[...], halo, kind_masks(sides[0:1, :], dofs)))
    for layer in range(layers):
        copies[layer].wait()
        factor = meta[2 * layers + layer : 2 * layers + layer + 1, :]
        kinds = meta[3 * layers + layer : 3 * layers + layer + 1, :]
        for piece in pieces(columns):
            masks = kind_masks(kinds[:, piece], dofs)
            for tracer in range(tracers):
                value = with_edges(g_in[layer, tracer, :, piece], fix, layer, tracer, tracers, piece, columns)
                if layer > 0:
                    value = value - factor[:, piece] * typed(
                        table[...], f_out[layer - 1, tracer, :, piece], masks
                    )
                f_out[layer, tracer, :, piece] = value
    width = columns // MEMBERS
    top = tracers * dofs
    for k, target in enumerate((m0, m1, m2, m3)):
        own = pl.ds(pl.multiple_of((place[0] ^ k) * width, width), width)
        for tracer in range(tracers):
            target[tracer * dofs : (tracer + 1) * dofs, :] = f_out[layers - 1, tracer, :, own]
        target[top : top + 2 * layers, :] = meta[0 : 2 * layers, own]
        target[top + 2 * layers : top + 3 * layers, :] = meta[3 * layers : 4 * layers, own]
        if target.shape[0] > top + 3 * layers:
            target[top + 3 * layers :, :] = jnp.zeros((target.shape[0] - top - 3 * layers, width), F32)


def local_backward_kernel(place, f_in, meta, table, m0, m1, m2, m3, carried):
    layers, tracers, dofs, columns = f_in.shape
    for layer in reversed(range(layers)):
        scale, inv_denom, kinds = (meta[i * layers + layer : i * layers + layer + 1, :] for i in (0, 1, 3))
        for piece in pieces(columns):
            masks = kind_masks(kinds[:, piece], dofs)
            for tracer in range(tracers):
                solved = f_in[layer, tracer, :, piece]
                if layer < layers - 1:
                    solved = solved - inv_denom[:, piece] * carried[tracer, :, piece]
                carried[tracer, :, piece] = scale[:, piece] * typed(table[...], solved, masks)
    width = columns // MEMBERS
    for k, target in enumerate((m0, m1, m2, m3)):
        own = pl.ds(pl.multiple_of((place[0] ^ k) * width, width), width)
        for tracer in range(tracers):
            target[tracer * dofs : (tracer + 1) * dofs, :] = carried[tracer, :, own]


def chain_rows(block_ref, top, layers, layer):
    def row(which):
        at = top + which * layers + layer
        return block_ref[at : at + 1, :]

    return row(0), row(1), row(2)


def forward_chain(turn, layers, tracers, table, blocks, entering, held):
    rows = entering.shape[1]
    dofs = rows // tracers
    parts = [slice(r * dofs, (r + 1) * dofs) for r in range(tracers)]
    if turn == 0:
        held[0] = jnp.zeros(held.shape[1:], F32)
        entering[1] = blocks[0, 0:rows, :]

    def step(block, carry):
        values = [entering[block, here, :] for here in parts]
        for layer in range(layers):
            scale, inv_denom, kinds = chain_rows(blocks.at[block], rows, layers, layer)
            masks = kind_masks(kinds, dofs)
            factor = -(scale * inv_denom)
            values = [factor * typed(table[...], v, masks) for v in values]
            for value, here in zip(values, parts):
                held[block, layer, here, :] = value
        for value, here in zip(values, parts):
            entering[block + 1, here, :] = value + blocks[block, here, :]
        return carry

    lax.fori_loop(1 if turn == 0 else 0, MEMBERS, step, 0)


def backward_chain(turn, layers, tracers, table, blocks, terms, returning, held):
    rows = returning.shape[1]
    dofs = rows // tracers
    parts = [slice(r * dofs, (r + 1) * dofs) for r in range(tracers)]

    def step(index, carry):
        block = MEMBERS - 1 - index
        values = [returning[block + 1, here, :] for here in parts]
        for layer in reversed(range(layers)):
            scale, inv_denom, kinds = chain_rows(blocks.at[block], rows, layers, layer)
            masks = kind_masks(kinds, dofs)
            values = [
                scale * typed(table[...], held[block, layer, here, :] - inv_denom * value, masks)
                for value, here in zip(values, parts)
            ]
        for value, here in zip(values, parts):
            returning[block, here, :] = value + terms[block, here, :]
        return carry

    lax.fori_loop(0, MEMBERS - 1 if turn == 0 else MEMBERS, step, 0)


def take(place, sources, target):
    for k, source in enumerate(sources):
        target[place[0] ^ k] = source[...]


def give(place, targets, source, first):
    for k, target in enumerate(targets):
        target[...] = source[first + (place[0] ^ k)]


def keep(place, turn, olds, targets):
    if olds:
        @pl.when(place[1] != turn)
        def passed():
            for old, target in zip(olds, targets):
                target[...] = old[...]


def chain_forward_kernel(turn, layers, tracers, place, inflow, table, m0, m1, m2, m3, *rest):
    olds, (states, o0, o1, o2, o3, outflow, blocks, entering) = rest[:-8], rest[-8:]
    outs = (o0, o1, o2, o3)

    @pl.when(place[1] == turn)
    def active():
        take(place, (m0, m1, m2, m3), blocks)
        entering[0] = inflow[...] if turn > 0 else jnp.zeros(inflow.shape, F32)
        forward_chain(turn, layers, tracers, table, blocks, entering, states)
        outflow[...] = entering[MEMBERS]
        give(place, outs, entering, 0)

    keep(place, turn, olds, outs)


def chain_last_kernel(
    turn, layers, tracers, place, inflow, up_table, down_table, m0, m1, m2, m3, e0, e1, e2, e3, *rest
):
    olds, (o0, o1, o2, o3, h0, h1, h2, h3, outflow, blocks, terms, entering, returning, held) = rest[:-14], rest[-14:]
    outs = (o0, o1, o2, o3)

    @pl.when(place[1] == turn)
    def active():
        take(place, (m0, m1, m2, m3), blocks)
        take(place, (e0, e1, e2, e3), terms)
        entering[0] = inflow[...] if turn > 0 else jnp.zeros(inflow.shape, F32)
        forward_chain(turn, layers, tracers, up_table, blocks, entering, held)
        returning[MEMBERS] = jnp.zeros(inflow.shape, F32)
        backward_chain(turn, layers, tracers, down_table, blocks, terms, returning, held)
        outflow[...] = returning[0]
        give(place, outs, entering, 0)
        give(place, (h0, h1, h2, h3), returning, 1)

    keep(place, turn, olds, outs)


def chain_backward_kernel(
    turn, layers, tracers, place, inflow, table, m0, m1, m2, m3, e0, e1, e2, e3, states, *rest
):
    olds, (o0, o1, o2, o3, outflow, blocks, terms, returning) = rest[:-8], rest[-8:]
    outs = (o0, o1, o2, o3)

    @pl.when(place[1] == turn)
    def active():
        take(place, (m0, m1, m2, m3), blocks)
        take(place, (e0, e1, e2, e3), terms)
        returning[MEMBERS] = inflow[...]
        backward_chain(turn, layers, tracers, table, blocks, terms, returning, states)
        outflow[...] = returning[0]
        give(place, outs, returning, 1)

    keep(place, turn, olds, outs)


def take_inflow(place, sources, state):
    tracers, dofs, columns = state.shape
    width = columns // MEMBERS
    for k, source in enumerate(sources):
        own = pl.ds(pl.multiple_of((place[0] ^ k) * width, width), width)
        for tracer in range(tracers):
            state[tracer, :, own] = source[tracer * dofs : (tracer + 1) * dofs, :]


def final_forward_kernel(place, f_in, meta, table, *rest):
    sources, (f_out, state) = rest[:-2], rest[-2:]
    layers, tracers, dofs, columns = f_in.shape
    take_inflow(place, sources, state)
    for layer in range(layers):
        factor, kinds = (meta[i * layers + layer : i * layers + layer + 1, :] for i in (2, 3))
        for piece in pieces(columns):
            masks = kind_masks(kinds[:, piece], dofs)
            for tracer in range(tracers):
                value = -(factor[:, piece] * typed(table[...], state[tracer, :, piece], masks))
                f_out[layer, tracer, :, piece] = f_in[layer, tracer, :, piece] + value
                if layer < layers - 1:
                    state[tracer, :, piece] = value


def final_backward_kernel(place, f_in, meta, table, *rest):
    sources, (out, carried, solved, sems) = rest[:-4], rest[-4:]
    layers, tracers, dofs, columns = f_in.shape
    take_inflow(place, sources, carried)
    copies = []
    for layer in reversed(range(layers)):
        scale, inv_denom, kinds = (meta[i * layers + layer : i * layers + layer + 1, :] for i in (0, 1, 3))
        for tracer in range(tracers):
            solved[layer, tracer] = f_in[layer, tracer] - inv_denom * carried[tracer]
            copies.append(
                pltpu.make_async_copy(
                    solved.at[layer, tracer], out.at[layer, tracer], sems.at[layer * tracers + tracer]
                )
            )
            copies[-1].start()
        if layer > 0:
            for piece in pieces(columns):
                masks = kind_masks(kinds[:, piece], dofs)
                for tracer in range(tracers):
                    carried[tracer, :, piece] = scale[:, piece] * typed(
                        table[...], solved[layer, tracer, :, piece], masks
                    )
    for copy in copies:
        copy.wait()


def per_device(rhs, lagged, kinds, stream, span, absorb, up, down, inverse):
    layers, tracers, dofs, columns = rhs.shape
    rows = tracers * dofs
    width = columns // MEMBERS
    count = lax.axis_size("stream")
    groups = count // MEMBERS
    position = lax.axis_index("stream")
    place = jnp.stack(
        [position % MEMBERS, position // MEMBERS, lax.axis_index("span") % 2]
    ).astype(jnp.int32)
    long_rows = rows + -(-3 * layers // 8) * 8
    vmem, anywhere, smem = (pl.BlockSpec(memory_space=s) for s in (pltpu.VMEM, pl.ANY, pltpu.SMEM))
    full = functools.partial(jax.ShapeDtypeStruct, dtype=F32)
    field = 4 * rhs.size
    product = 2 * KINDS * dofs * 4 * dofs * tracers * columns
    some = 12 << 20
    table_shape = (KINDS * dofs, 4 * dofs)
    fix = full((dofs, 128))

    def exchanged(messages):
        return [messages[0]] + [
            lax.ppermute(messages[k], "stream", [(i, i ^ k) for i in range(count)])
            for k in range(1, MEMBERS)
        ]

    def between(values, step):
        pairs = [(step * MEMBERS + i, (step + 1) * MEMBERS + i) for i in range(MEMBERS)]
        return lax.ppermute(values, "stream", pairs + [(b, a) for a, b in pairs])

    column_state = pltpu.VMEM((tracers, dofs, columns), F32)
    message = full((rows, width))
    long_message = full((long_rows, width))
    table = jax.ShapeDtypeStruct(table_shape, BF16)
    inputs = (rhs, lagged, kinds, stream, span, absorb, up, down, inverse)

    g, meta, sides, edges, up_table, down_table = pl.pallas_call(
        span_kernel,
        out_shape=(
            pltpu.HBM(rhs.shape, F32), full((4 * layers, columns)), full((8, 128)), fix, table, table,
        ),
        in_specs=[anywhere] * len(inputs),
        out_specs=(anywhere,) + (vmem,) * 5,
        scratch_shapes=[pltpu.VMEM((dofs, 4 * dofs), BF16), pltpu.VMEM(rhs.shape, F32)]
        + [pltpu.VMEM(value.shape, value.dtype) for value in inputs]
        + [pltpu.SemaphoreType.DMA((2 * layers + 7,)), pltpu.SemaphoreType.DMA((layers,))],
        name="span_terms",
        **params(2 * layers * product, 3 * field, some + 4 * field),
    )(*(pltpu.with_memory_space_constraint(value, pltpu.HBM) for value in inputs))

    across = lax.axis_size("span")
    crossing = [(i, i + 1) for i in range(1, across - 1, 2)]
    pair = lax.ppermute(edges, "span", [(i, i ^ 1) for i in range(across)])
    cross = lax.ppermute(edges, "span", crossing + [(b, a) for a, b in crossing])

    f_zero, *out_b = pl.pallas_call(
        local_forward_kernel,
        out_shape=(full(rhs.shape),) + (long_message,) * MEMBERS,
        in_specs=[smem, vmem, vmem, anywhere] + [vmem] * 3,
        out_specs=(vmem,) * (1 + MEMBERS),
        scratch_shapes=[pltpu.VMEM(rhs.shape, F32), pltpu.SemaphoreType.DMA((layers,))],
        name="local_forward",
        **params(layers * product, field, some + 2 * field),
    )(place, pair, cross, pltpu.with_memory_space_constraint(g, pltpu.HBM), meta, sides, up_table)
    in_b = exchanged(out_b)

    out_e = pl.pallas_call(
        local_backward_kernel,
        out_shape=(message,) * MEMBERS,
        in_specs=[smem] + [vmem] * 3,
        out_specs=(vmem,) * MEMBERS,
        scratch_shapes=[column_state],
        name="local_backward",
        **params(layers * product, field, some + field),
    )(place, f_zero, meta, down_table)
    in_e = exchanged(out_e)
    in_b, _ = lax.optimization_barrier((in_b, out_e))

    blocks = pltpu.VMEM((MEMBERS, long_rows, width), F32)
    inner = pltpu.VMEM((MEMBERS + 1, rows, width), F32)
    held = (MEMBERS, layers, rows, width)
    inflow = jnp.zeros((rows, width), F32)
    states, out_f = [], []
    for turn in range(groups - 1):
        state, *out_f, outflow = pl.pallas_call(
            functools.partial(chain_forward_kernel, turn, layers, tracers),
            out_shape=(full(held),) + (message,) * (MEMBERS + 1),
            in_specs=[smem] + [vmem] * (2 + MEMBERS + len(out_f)),
            out_specs=(vmem,) * (MEMBERS + 2),
            scratch_shapes=[blocks, inner],
            name=f"chain_forward_{turn}",
            **params(layers * product, 2 * field, some + field),
        )(place, inflow, up_table, *in_b, *out_f)
        states.append(state)
        inflow = between(outflow, turn)

    *out_f, h0, h1, h2, h3, outflow = pl.pallas_call(
        functools.partial(chain_last_kernel, groups - 1, layers, tracers),
        out_shape=(message,) * (2 * MEMBERS + 1),
        in_specs=[smem] + [vmem] * (3 + 2 * MEMBERS + len(out_f)),
        out_specs=(vmem,) * (2 * MEMBERS + 1),
        scratch_shapes=[blocks, inner, inner, inner, pltpu.VMEM(held, F32)],
        name="chain_last",
        **params(2 * layers * product, 2 * field, some + 2 * field),
    )(place, inflow, up_table, down_table, *in_b, *in_e, *out_f)
    in_f = exchanged(out_f)
    out_h = [h0, h1, h2, h3]

    for turn in reversed(range(groups - 1)):
        inflow = between(outflow, turn)
        *out_h, outflow = pl.pallas_call(
            functools.partial(chain_backward_kernel, turn, layers, tracers),
            out_shape=(message,) * (MEMBERS + 1),
            in_specs=[smem] + [vmem] * (3 + 3 * MEMBERS),
            out_specs=(vmem,) * (MEMBERS + 1),
            scratch_shapes=[blocks, inner, inner],
            name=f"chain_backward_{turn}",
            **params(layers * product, 2 * field, some + field),
        )(place, inflow, down_table, *in_b, *in_e, states[turn], *out_h)
    in_h = exchanged(out_h)

    f_part = pl.pallas_call(
        final_forward_kernel,
        out_shape=full(rhs.shape),
        in_specs=[smem] + [vmem] * (3 + len(in_f)),
        out_specs=vmem,
        scratch_shapes=[column_state],
        name="final_forward",
        **params(layers * product, 2 * field, some + 2 * field),
    )(place, f_zero, meta, up_table, *in_f)
    return pl.pallas_call(
        final_backward_kernel,
        out_shape=full(rhs.shape),
        in_specs=[smem] + [vmem] * (3 + len(in_h)),
        out_specs=anywhere,
        scratch_shapes=[
            column_state,
            pltpu.VMEM(rhs.shape, F32),
            pltpu.SemaphoreType.DMA((layers * tracers,)),
        ],
        name="final_backward",
        **params(layers * product, 2 * field, some + 2 * field),
    )(place, f_part, meta, down_table, *in_h)


def solution(mesh):
    return jax.shard_map(
        per_device,
        mesh=mesh,
        in_specs=(
            P("stream", None, None, "span"),
            P("stream", None, None, "span"),
            P(None, "stream", "span"),
            P("stream", "span"),
            P(None, "stream", "span"),
            P("stream", "span"),
            P(),
            P(),
            P(),
        ),
        out_specs=P("stream", None, None, "span"),
        check_vma=False,
    )
```

```python
import functools

import jax
import jax.numpy as jnp
from jax import lax
from jax.experimental import pallas as pl
from jax.experimental.pallas import tpu as pltpu
from jax.sharding import PartitionSpec as P

KINDS = 6
MEMBERS = 4
PIECE = 256
F32 = jnp.float32
BF16 = jnp.bfloat16


def parts_of(value):
    high = value.astype(BF16)
    low = (value - high.astype(F32)).astype(BF16)
    return high, low


def stacked_state(value):
    high, low = parts_of(value)
    return jnp.concatenate([high, low, high, low], axis=0)


def stacked_table(value):
    high, low = parts_of(value)
    return jnp.concatenate([high, high, low, low], axis=1)


def kind_masks(kinds_row, rows):
    wide = jnp.broadcast_to(kinds_row, (rows, kinds_row.shape[1]))
    return [wide == t for t in range(1, KINDS)]


def select(products, masks):
    rows = products.shape[0] // KINDS
    chosen = products[:rows]
    for t in range(1, KINDS):
        chosen = jnp.where(masks[t - 1], products[t * rows : (t + 1) * rows], chosen)
    return chosen


def typed(table, state, masks):
    return select(jnp.dot(table, stacked_state(state), preferred_element_type=F32), masks)


def params(flops, moved, vmem):
    return dict(
        compiler_params=pltpu.CompilerParams(vmem_limit_bytes=vmem),
        cost_estimate=pl.CostEstimate(flops=flops, bytes_accessed=moved, transcendentals=0),
    )


def pieces(columns):
    return [slice(at, at + PIECE) for at in range(0, columns, PIECE)]


def fold_table(inverse, source, target):
    dofs = inverse.shape[0]
    dinv = inverse[...]
    for t in range(KINDS):
        folded = jnp.dot(dinv, source[t], preferred_element_type=F32, precision=lax.Precision.HIGHEST)
        target[t * dofs : (t + 1) * dofs, :] = stacked_table(folded)


def span_kernel(
    place, rhs, lagged, kinds, stream, span, absorb, up, inverse,
    g_out, meta, sides, edges, up_table,
    inv_table, rhs_in, lagged_in, kinds_in, stream_in, span_in, absorb_in, ups, inv, sems,
):
    layers, tracers, dofs, columns = g_out.shape
    small = [
        pltpu.make_async_copy(source, target, sems.at[2 * layers + i])
        for i, (source, target) in enumerate(
            (
                (up, ups), (inverse, inv),
                (kinds, kinds_in), (stream, stream_in), (span, span_in), (absorb, absorb_in),
            )
        )
    ]

    def loads(layer):
        return (
            pltpu.make_async_copy(lagged.at[layer], lagged_in.at[layer], sems.at[2 * layer]),
            pltpu.make_async_copy(rhs.at[layer], rhs_in.at[layer], sems.at[2 * layer + 1]),
        )

    for copy in small:
        copy.start()
    for layer in range(layers):
        for copy in loads(layer):
            copy.start()
    for copy in small:
        copy.wait()
    fold_table(inv, ups, up_table)
    inv_table[...] = stacked_table(inv[...])
    scales = stream_in[...]
    inv_denoms = 1.0 / (scales + span_in[0] + span_in[1] + absorb_in[...])
    for i, rows in enumerate((scales, inv_denoms, scales * inv_denoms, kinds_in[0].astype(F32))):
        meta[i * layers : (i + 1) * layers, :] = rows
    lane = lax.broadcasted_iota(jnp.int32, (1, 128), 1)
    wide_lane = lax.broadcasted_iota(jnp.int32, (1, columns), 1)
    sides[...] = jnp.zeros(sides.shape, F32)
    edges[...] = jnp.zeros(edges.shape, F32)

    def step(layer):
        row = slice(layer, layer + 1)
        inv_denom = inv_denoms[row]
        weight_low = inv_denom * span_in[0, row, :]
        weight_high = inv_denom * span_in[1, row, :]
        kinds_low = kinds_in[1, row, :]
        kinds_high = kinds_in[2, row, :]
        for side, weight, kind, at in (
            (0, weight_low, kinds_low, 0),
            (1, weight_high, kinds_high, columns - 1),
        ):
            here = lane // tracers == 2 * layer + side
            sides[0:1, :] = jnp.where(here, kind[:, at : at + 1].astype(F32), sides[0:1, :])
            sides[1:2, :] = jnp.where(here, weight[:, at : at + 1], sides[1:2, :])
        weight_low = jnp.where(wide_lane == 0, 0.0, weight_low)
        weight_high = jnp.where(wide_lane == columns - 1, 0.0, weight_high)
        kinds_low = pltpu.roll(kinds_low, columns - 1, 1)
        kinds_high = pltpu.roll(kinds_high, 1, 1)
        for copy in loads(layer):
            copy.wait()
        edge_values = edges[...]
        for tracer in range(tracers):
            for side, at in ((0, 0), (1, columns - 1)):
                here = lane == side * 64 + layer * 2 * tracers + tracer
                edge_values = jnp.where(here, lagged_in[layer, tracer, :, at : at + 1], edge_values)
        edges[...] = edge_values
        for tracer in range(tracers):
            lows, highs, solved = [], [], []
            for piece in pieces(columns):
                products = jnp.dot(
                    up_table[...], stacked_state(lagged_in[layer, tracer, :, piece]), preferred_element_type=F32
                )
                lows.append(select(products, kind_masks(kinds_low[:, piece], dofs)))
                highs.append(select(products, kind_masks(kinds_high[:, piece], dofs)))
                solved.append(
                    jnp.dot(
                        inv_table[...], stacked_state(rhs_in[layer, tracer, :, piece]), preferred_element_type=F32
                    )
                )
            low_term = pltpu.roll(jnp.concatenate(lows, axis=1), 1, 1)
            high_term = pltpu.roll(jnp.concatenate(highs, axis=1), columns - 1, 1)
            g_out[layer, tracer] = (
                inv_denom * jnp.concatenate(solved, axis=1) - weight_low * low_term - weight_high * high_term
            )

    for layer in range(layers):
        step(layer)


def own_columns(place, k, width):
    return pl.ds(pl.multiple_of((place[0] ^ k) * width, width), width)


def meta_rows(meta, own, layers, layer):
    return [meta[i * layers + layer : i * layers + layer + 1, own] for i in range(4)]


def edge_value(fix, layer, tracer, tracers, side):
    lane = lax.broadcasted_iota(jnp.int32, (1, 128), 1)
    at = (2 * layer + side) * tracers + tracer
    return jnp.where(lane == (127 if side else 0), fix[:, at : at + 1], 0.0)


def with_edges(value, fix, layer, tracer, tracers, piece, columns):
    if piece.start == 0:
        low = value[:, :128] + edge_value(fix, layer, tracer, tracers, 0)
        value = jnp.concatenate([low, value[:, 128:]], axis=1)
    if piece.stop == columns:
        end = value.shape[1] - 128
        high = value[:, end:] + edge_value(fix, layer, tracer, tracers, 1)
        value = jnp.concatenate([value[:, :end], high], axis=1)
    return value


def local_forward_kernel(
    place, pair, cross, g_in, meta, sides, table, f_out, m0, m1, m2, m3
):
    layers, tracers, dofs, columns = g_in.shape
    odd = place[2] == 1
    from_low = pltpu.roll(jnp.where(odd, pair[...], cross[...]), 64, 1)
    from_high = pltpu.roll(jnp.where(odd, cross[...], pair[...]), tracers, 1)
    lane = lax.broadcasted_iota(jnp.int32, (1, 128), 1)
    halo = jnp.where(lane % (2 * tracers) < tracers, from_low, from_high)
    fix = -(sides[1:2, :] * typed(table[...], halo, kind_masks(sides[0:1, :], dofs)))
    for layer in range(layers):
        factor = meta[2 * layers + layer : 2 * layers + layer + 1, :]
        kinds = meta[3 * layers + layer : 3 * layers + layer + 1, :]
        for piece in pieces(columns):
            masks = kind_masks(kinds[:, piece], dofs)
            for tracer in range(tracers):
                value = with_edges(g_in[layer, tracer, :, piece], fix, layer, tracer, tracers, piece, columns)
                if layer > 0:
                    value = value - factor[:, piece] * typed(
                        table[...], f_out[layer - 1, tracer, :, piece], masks
                    )
                f_out[layer, tracer, :, piece] = value
    width = columns // MEMBERS
    top = tracers * dofs
    for k, target in enumerate((m0, m1, m2, m3)):
        own = pl.ds(pl.multiple_of((place[0] ^ k) * width, width), width)
        for tracer in range(tracers):
            target[tracer * dofs : (tracer + 1) * dofs, :] = f_out[layers - 1, tracer, :, own]
        target[top : top + 2 * layers, :] = meta[0 : 2 * layers, own]
        target[top + 2 * layers : top + 3 * layers, :] = meta[3 * layers : 4 * layers, own]
        if target.shape[0] > top + 3 * layers:
            target[top + 3 * layers :, :] = jnp.zeros((target.shape[0] - top - 3 * layers, width), F32)


def local_backward_kernel(
    place, f_in, meta, down, inverse, table, m0, m1, m2, m3, carried, downs, inv, sems
):
    copies = [
        pltpu.make_async_copy(source, target, sems.at[i])
        for i, (source, target) in enumerate(((down, downs), (inverse, inv)))
    ]
    for copy in copies:
        copy.start()
    for copy in copies:
        copy.wait()
    fold_table(inv, downs, table)
    layers, tracers, dofs, columns = f_in.shape
    for layer in reversed(range(layers)):
        scale, inv_denom, kinds = (meta[i * layers + layer : i * layers + layer + 1, :] for i in (0, 1, 3))
        for piece in pieces(columns):
            masks = kind_masks(kinds[:, piece], dofs)
            for tracer in range(tracers):
                solved = f_in[layer, tracer, :, piece]
                if layer < layers - 1:
                    solved = solved - inv_denom[:, piece] * carried[tracer, :, piece]
                carried[tracer, :, piece] = scale[:, piece] * typed(table[...], solved, masks)
    width = columns // MEMBERS
    for k, target in enumerate((m0, m1, m2, m3)):
        own = pl.ds(pl.multiple_of((place[0] ^ k) * width, width), width)
        for tracer in range(tracers):
            target[tracer * dofs : (tracer + 1) * dofs, :] = carried[tracer, :, own]


def chain_rows(block_ref, top, layers, layer):
    def row(which):
        at = top + which * layers + layer
        return block_ref[at : at + 1, :]

    return row(0), row(1), row(2)


def forward_chain(turn, layers, tracers, table, blocks, entering, held):
    rows = entering.shape[1]
    dofs = rows // tracers
    parts = [slice(r * dofs, (r + 1) * dofs) for r in range(tracers)]
    if turn == 0:
        held[0] = jnp.zeros(held.shape[1:], F32)
        entering[1] = blocks[0, 0:rows, :]

    def step(block, carry):
        values = [entering[block, here, :] for here in parts]
        for layer in range(layers):
            scale, inv_denom, kinds = chain_rows(blocks.at[block], rows, layers, layer)
            masks = kind_masks(kinds, dofs)
            factor = -(scale * inv_denom)
            values = [factor * typed(table[...], v, masks) for v in values]
            for value, here in zip(values, parts):
                held[block, layer, here, :] = value
        for value, here in zip(values, parts):
            entering[block + 1, here, :] = value + blocks[block, here, :]
        return carry

    lax.fori_loop(1 if turn == 0 else 0, MEMBERS, step, 0)


def backward_chain(turn, layers, tracers, table, blocks, terms, returning, held):
    rows = returning.shape[1]
    dofs = rows // tracers
    parts = [slice(r * dofs, (r + 1) * dofs) for r in range(tracers)]

    def step(index, carry):
        block = MEMBERS - 1 - index
        values = [returning[block + 1, here, :] for here in parts]
        for layer in reversed(range(layers)):
            scale, inv_denom, kinds = chain_rows(blocks.at[block], rows, layers, layer)
            masks = kind_masks(kinds, dofs)
            values = [
                scale * typed(table[...], held[block, layer, here, :] - inv_denom * value, masks)
                for value, here in zip(values, parts)
            ]
        for value, here in zip(values, parts):
            returning[block, here, :] = value + terms[block, here, :]
        return carry

    lax.fori_loop(0, MEMBERS - 1 if turn == 0 else MEMBERS, step, 0)


def take(place, sources, target, top=0):
    for k, source in enumerate(sources):
        target[place[0] ^ k, top:, :] = source[top:, :]


def give(place, targets, source, first):
    for k, target in enumerate(targets):
        target[...] = source[first + (place[0] ^ k)]


def keep(place, turn, olds, targets):
    if olds:
        @pl.when(place[1] != turn)
        def passed():
            for old, target in zip(olds, targets):
                target[...] = old[...]


def chain_forward_kernel(turn, layers, tracers, place, inflow, table, m0, m1, m2, m3, *rest):
    olds, (states, o0, o1, o2, o3, outflow, blocks, entering) = rest[:-8], rest[-8:]
    outs = (o0, o1, o2, o3)

    @pl.when(place[1] == turn)
    def active():
        take(place, (m0, m1, m2, m3), blocks)
        entering[0] = inflow[...] if turn > 0 else jnp.zeros(inflow.shape, F32)
        forward_chain(turn, layers, tracers, table, blocks, entering, states)
        outflow[...] = entering[MEMBERS]
        give(place, outs, entering, 0)

    keep(place, turn, olds, outs)


def chain_last_kernel(
    turn, layers, tracers, place, inflow, up_table, down_table, m0, m1, m2, m3, e0, e1, e2, e3, *rest
):
    olds, (o0, o1, o2, o3, h0, h1, h2, h3, outflow, blocks, terms, entering, returning, held) = rest[:-14], rest[-14:]
    outs = (o0, o1, o2, o3)

    @pl.when(place[1] == turn)
    def active():
        take(place, (m0, m1, m2, m3), blocks)
        take(place, (e0, e1, e2, e3), terms)
        entering[0] = inflow[...] if turn > 0 else jnp.zeros(inflow.shape, F32)
        forward_chain(turn, layers, tracers, up_table, blocks, entering, held)
        returning[MEMBERS] = jnp.zeros(inflow.shape, F32)
        backward_chain(turn, layers, tracers, down_table, blocks, terms, returning, held)
        outflow[...] = returning[0]
        give(place, outs, entering, 0)
        give(place, (h0, h1, h2, h3), returning, 1)

    keep(place, turn, olds, outs)


def chain_backward_kernel(
    turn, layers, tracers, place, inflow, table, m0, m1, m2, m3, e0, e1, e2, e3, states, *rest
):
    olds, (o0, o1, o2, o3, outflow, blocks, terms, returning) = rest[:-8], rest[-8:]
    outs = (o0, o1, o2, o3)

    @pl.when(place[1] == turn)
    def active():
        take(place, (m0, m1, m2, m3), blocks, returning.shape[1])
        take(place, (e0, e1, e2, e3), terms)
        returning[MEMBERS] = inflow[...]
        backward_chain(turn, layers, tracers, table, blocks, terms, returning, states)
        outflow[...] = returning[0]
        give(place, outs, returning, 1)

    keep(place, turn, olds, outs)


def final_forward_kernel(place, f_in, meta, table, m0, m1, m2, m3, f_out, state):
    _, layers, tracers, dofs, width = f_out.shape
    for layer in range(layers):
        for k, message in enumerate((m0, m1, m2, m3)):
            own = own_columns(place, k, width)
            factor, kinds = meta_rows(meta, own, layers, layer)[2:]
            masks = kind_masks(kinds, dofs)
            for tracer in range(tracers):
                here = slice(tracer * dofs, (tracer + 1) * dofs)
                before = message[here, :] if layer == 0 else state[k, tracer]
                value = -(factor * typed(table[...], before, masks))
                f_out[k, layer, tracer] = f_in[layer, tracer, :, own] + value
                if layer < layers - 1:
                    state[k, tracer] = value


def final_backward_kernel(ks, place, f_in, meta, table, *rest):
    messages = rest[: len(ks)]
    out, carried, solved, sems = rest[-4:]
    _, layers, tracers, dofs, width = f_in.shape
    copies = []
    for layer in reversed(range(layers)):
        for i, (k, message) in enumerate(zip(ks, messages)):
            own = own_columns(place, k, width)
            scale, inv_denom, _, kinds = meta_rows(meta, own, layers, layer)
            masks = kind_masks(kinds, dofs)
            for tracer in range(tracers):
                here = slice(tracer * dofs, (tracer + 1) * dofs)
                before = message[here, :] if layer == layers - 1 else carried[i, tracer]
                solved[i, layer, tracer] = f_in[k, layer, tracer] - inv_denom * before
            copies.append(
                pltpu.make_async_copy(solved.at[i, layer], out.at[layer, :, :, own], sems.at[i, layer])
            )
            copies[-1].start()
            if layer > 0:
                for tracer in range(tracers):
                    carried[i, tracer] = scale * typed(table[...], solved[i, layer, tracer], masks)
    for copy in copies:
        copy.wait()


def per_device(rhs, lagged, kinds, stream, span, absorb, up, down, inverse):
    layers, tracers, dofs, columns = rhs.shape
    rows = tracers * dofs
    width = columns // MEMBERS
    count = lax.axis_size("stream")
    groups = count // MEMBERS
    position = lax.axis_index("stream")
    place = jnp.stack(
        [position % MEMBERS, position // MEMBERS, lax.axis_index("span") % 2]
    ).astype(jnp.int32)
    long_rows = rows + -(-3 * layers // 8) * 8
    vmem, anywhere, smem = (pl.BlockSpec(memory_space=s) for s in (pltpu.VMEM, pl.ANY, pltpu.SMEM))
    full = functools.partial(jax.ShapeDtypeStruct, dtype=F32)
    field = 4 * rhs.size
    product = 2 * KINDS * dofs * 4 * dofs * tracers * columns
    some = 12 << 20
    table_shape = (KINDS * dofs, 4 * dofs)
    fix = full((dofs, 128))

    def sent(value, k):
        return lax.ppermute(value, "stream", [(i, i ^ k) for i in range(count)]) if k else value

    def exchanged(messages):
        return [sent(value, k) for k, value in enumerate(messages)]

    def between(values, step):
        pairs = [(step * MEMBERS + i, (step + 1) * MEMBERS + i) for i in range(MEMBERS)]
        return lax.ppermute(values, "stream", pairs + [(b, a) for a, b in pairs])

    piece = (layers, tracers, dofs, width)
    early, late = tuple(range(MEMBERS - 1)), (MEMBERS - 1,)
    message = full((rows, width))
    long_message = full((long_rows, width))
    table = jax.ShapeDtypeStruct(table_shape, BF16)
    inputs = (rhs, lagged, kinds, stream, span, absorb, up, inverse)

    g, meta, sides, edges, up_table = pl.pallas_call(
        span_kernel,
        out_shape=(
            full(rhs.shape), full((4 * layers, columns)), full((8, 128)), fix, table,
        ),
        in_specs=[smem] + [anywhere] * len(inputs),
        out_specs=(vmem,) * 5,
        scratch_shapes=[pltpu.VMEM((dofs, 4 * dofs), BF16)]
        + [pltpu.VMEM(value.shape, value.dtype) for value in inputs]
        + [pltpu.SemaphoreType.DMA((2 * layers + 6,))],
        name="span_terms",
        **params(1 << 10, 1 << 10, some + 3 * field),
    )(place, *(pltpu.with_memory_space_constraint(value, pltpu.HBM) for value in inputs))

    across = lax.axis_size("span")
    crossing = [(i, i + 1) for i in range(1, across - 1, 2)]
    pair = lax.ppermute(edges, "span", [(i, i ^ 1) for i in range(across)])
    cross = lax.ppermute(edges, "span", crossing + [(b, a) for a, b in crossing])

    def piece_scratch(ks):
        return [pltpu.VMEM((len(ks), *piece), F32), pltpu.SemaphoreType.DMA((len(ks), layers))]

    f_zero, *out_b = pl.pallas_call(
        local_forward_kernel,
        out_shape=(full(rhs.shape),) + (long_message,) * MEMBERS,
        in_specs=[smem] + [vmem] * 6,
        out_specs=(vmem,) * (1 + MEMBERS),
        name="local_forward",
        **params(1 << 10, 1 << 10, some + field),
    )(place, pair, cross, g, meta, sides, up_table)
    in_b = exchanged(out_b)

    down_table, *out_e = pl.pallas_call(
        local_backward_kernel,
        out_shape=(table,) + (message,) * MEMBERS,
        in_specs=[smem] + [vmem] * 2 + [anywhere] * 2,
        out_specs=(vmem,) * (1 + MEMBERS),
        scratch_shapes=[
            pltpu.VMEM((tracers, dofs, columns), F32), pltpu.VMEM(down.shape, F32),
            pltpu.VMEM(inverse.shape, F32), pltpu.SemaphoreType.DMA((2,)),
        ],
        name="local_backward",
        **params(1 << 10, 1 << 10, some + field),
    )(place, f_zero, meta, *(pltpu.with_memory_space_constraint(value, pltpu.HBM) for value in (down, inverse)))
    in_e = exchanged(out_e)
    in_b, _ = lax.optimization_barrier((in_b, out_e))

    blocks = pltpu.VMEM((MEMBERS, long_rows, width), F32)
    inner = pltpu.VMEM((MEMBERS + 1, rows, width), F32)
    held = (MEMBERS, layers, rows, width)
    inflow = out_e[0]
    states, out_f = [], []
    for turn in range(groups - 1):
        state, *out_f, outflow = pl.pallas_call(
            functools.partial(chain_forward_kernel, turn, layers, tracers),
            out_shape=(full(held),) + (message,) * (MEMBERS + 1),
            in_specs=[smem] + [vmem] * (2 + MEMBERS + len(out_f)),
            out_specs=(vmem,) * (MEMBERS + 2),
            scratch_shapes=[blocks, inner],
            name=f"chain_forward_{turn}",
            **params(1 << 10, 1 << 10, some + field),
        )(place, inflow, up_table, *in_b, *out_f)
        states.append(state)
        inflow = between(outflow, turn)

    *out_f, h0, h1, h2, h3, outflow = pl.pallas_call(
        functools.partial(chain_last_kernel, groups - 1, layers, tracers),
        out_shape=(message,) * (2 * MEMBERS + 1),
        in_specs=[smem] + [vmem] * (3 + 2 * MEMBERS + len(out_f)),
        out_specs=(vmem,) * (2 * MEMBERS + 1),
        scratch_shapes=[blocks, inner, inner, inner, pltpu.VMEM(held, F32)],
        name="chain_last",
        **params(1 << 10, 1 << 10, some + 2 * field),
    )(place, inflow, up_table, down_table, *in_b, *in_e, *out_f)
    in_f = exchanged(out_f)
    out_h = [h0, h1, h2, h3]

    for turn in reversed(range(groups - 1)):
        inflow = between(outflow, turn)
        *out_h, outflow = pl.pallas_call(
            functools.partial(chain_backward_kernel, turn, layers, tracers),
            out_shape=(message,) * (MEMBERS + 1),
            in_specs=[smem] + [vmem] * (3 + 3 * MEMBERS),
            out_specs=(vmem,) * (MEMBERS + 1),
            scratch_shapes=[blocks, inner, inner],
            name=f"chain_backward_{turn}",
            **params(1 << 10, 1 << 10, some + field),
        )(place, inflow, down_table, *in_b, *in_e, states[turn], *out_h)
    in_h = exchanged(out_h)

    f_part = pl.pallas_call(
        final_forward_kernel,
        out_shape=full((MEMBERS, *piece)),
        in_specs=[smem] + [vmem] * (3 + MEMBERS),
        out_specs=vmem,
        scratch_shapes=[pltpu.VMEM((MEMBERS, tracers, dofs, width), F32)],
        name="final_forward",
        **params(1 << 10, 1 << 10, some + 2 * field),
    )(place, f_zero, meta, up_table, *in_f)
    out = ()
    for ks in (early, late):
        out = (
            pl.pallas_call(
                functools.partial(final_backward_kernel, ks),
                out_shape=full(rhs.shape),
                in_specs=[smem] + [vmem] * (3 + len(ks)) + [anywhere] * len(out),
                out_specs=anywhere,
                scratch_shapes=[pltpu.VMEM((len(ks), tracers, dofs, width), F32)] + piece_scratch(ks),
                input_output_aliases={4 + len(ks): 0} if out else {},
                name=f"final_backward_{ks[0]}",
                **params(1 << 10, 1 << 10, some + field),
            )(place, f_part, meta, down_table, *(in_h[k] for k in ks), *out),
        )
    return out[0]


def solution(mesh):
    return jax.shard_map(
        per_device,
        mesh=mesh,
        in_specs=(
            P("stream", None, None, "span"),
            P("stream", None, None, "span"),
            P(None, "stream", "span"),
            P("stream", "span"),
            P(None, "stream", "span"),
            P("stream", "span"),
            P(),
            P(),
            P(),
        ),
        out_specs=P("stream", None, None, "span"),
        check_vma=False,
    )
```

```python
import functools

import jax
import jax.numpy as jnp
from jax import lax
from jax.experimental import pallas as pl
from jax.experimental.pallas import tpu as pltpu
from jax.sharding import PartitionSpec as P

KINDS = 6
MEMBERS = 4
PIECE = 256
F32 = jnp.float32
BF16 = jnp.bfloat16


def parts_of(value):
    high = value.astype(BF16)
    low = (value - high.astype(F32)).astype(BF16)
    return high, low


def stacked_state(value):
    high, low = parts_of(value)
    return jnp.concatenate([high, low, high], axis=0)


def stacked_table(value):
    high, low = parts_of(value)
    return jnp.concatenate([high, high, low], axis=1)


def kind_masks(kinds_row, rows):
    wide = jnp.broadcast_to(kinds_row, (rows, kinds_row.shape[1]))
    return [wide == t for t in range(1, KINDS)]


def select(products, masks):
    rows = products.shape[0] // KINDS
    chosen = products[:rows]
    for t in range(1, KINDS):
        chosen = jnp.where(masks[t - 1], products[t * rows : (t + 1) * rows], chosen)
    return chosen


def typed(table, state, masks):
    return select(jnp.dot(table, stacked_state(state), preferred_element_type=F32), masks)


def params(flops, moved, vmem):
    return dict(
        compiler_params=pltpu.CompilerParams(vmem_limit_bytes=vmem),
        cost_estimate=pl.CostEstimate(flops=flops, bytes_accessed=moved, transcendentals=0),
    )


def pieces(columns):
    return [slice(at, at + PIECE) for at in range(0, columns, PIECE)]


def fold_table(inverse, source, target):
    dofs = inverse.shape[0]
    dinv = inverse[...]
    for t in range(KINDS):
        folded = jnp.dot(dinv, source[t], preferred_element_type=F32, precision=lax.Precision.HIGHEST)
        target[t * dofs : (t + 1) * dofs, :] = stacked_table(folded)


def span_kernel(
    place, rhs, lagged, kinds, stream, span, absorb, up, inverse,
    g_out, meta, sides, edges, up_table,
    inv_table, rhs_in, lagged_in, kinds_in, stream_in, span_in, absorb_in, ups, inv, sems,
):
    layers, tracers, dofs, columns = g_out.shape
    small = [
        pltpu.make_async_copy(source, target, sems.at[2 * layers + i])
        for i, (source, target) in enumerate(
            (
                (up, ups), (inverse, inv),
                (kinds, kinds_in), (stream, stream_in), (span, span_in), (absorb, absorb_in),
            )
        )
    ]

    def loads(layer):
        return (
            pltpu.make_async_copy(lagged.at[layer], lagged_in.at[layer], sems.at[2 * layer]),
            pltpu.make_async_copy(rhs.at[layer], rhs_in.at[layer], sems.at[2 * layer + 1]),
        )

    for copy in small:
        copy.start()
    for layer in range(layers):
        for copy in loads(layer):
            copy.start()
    for copy in small:
        copy.wait()
    fold_table(inv, ups, up_table)
    inv_table[...] = stacked_table(inv[...])
    scales = stream_in[...]
    inv_denoms = 1.0 / (scales + span_in[0] + span_in[1] + absorb_in[...])
    for i, rows in enumerate((scales, inv_denoms, scales * inv_denoms, kinds_in[0].astype(F32))):
        meta[i * layers : (i + 1) * layers, :] = rows
    lane = lax.broadcasted_iota(jnp.int32, (1, 128), 1)
    wide_lane = lax.broadcasted_iota(jnp.int32, (1, columns), 1)
    sides[...] = jnp.zeros(sides.shape, F32)
    edges[...] = jnp.zeros(edges.shape, F32)

    def step(layer):
        row = slice(layer, layer + 1)
        inv_denom = inv_denoms[row]
        weight_low = inv_denom * span_in[0, row, :]
        weight_high = inv_denom * span_in[1, row, :]
        kinds_low = kinds_in[1, row, :]
        kinds_high = kinds_in[2, row, :]
        for side, weight, kind, at in (
            (0, weight_low, kinds_low, 0),
            (1, weight_high, kinds_high, columns - 1),
        ):
            here = lane // tracers == 2 * layer + side
            sides[0:1, :] = jnp.where(here, kind[:, at : at + 1].astype(F32), sides[0:1, :])
            sides[1:2, :] = jnp.where(here, weight[:, at : at + 1], sides[1:2, :])
        weight_low = jnp.where(wide_lane == 0, 0.0, weight_low)
        weight_high = jnp.where(wide_lane == columns - 1, 0.0, weight_high)
        kinds_low = pltpu.roll(kinds_low, columns - 1, 1)
        kinds_high = pltpu.roll(kinds_high, 1, 1)
        for copy in loads(layer):
            copy.wait()
        edge_values = edges[...]
        for tracer in range(tracers):
            for side, at in ((0, 0), (1, columns - 1)):
                here = lane == side * 64 + layer * 2 * tracers + tracer
                edge_values = jnp.where(here, lagged_in[layer, tracer, :, at : at + 1], edge_values)
        edges[...] = edge_values
        for tracer in range(tracers):
            lows, highs, solved = [], [], []
            for piece in pieces(columns):
                products = jnp.dot(
                    up_table[...], stacked_state(lagged_in[layer, tracer, :, piece]), preferred_element_type=F32
                )
                lows.append(select(products, kind_masks(kinds_low[:, piece], dofs)))
                highs.append(select(products, kind_masks(kinds_high[:, piece], dofs)))
                solved.append(
                    jnp.dot(
                        inv_table[...], stacked_state(rhs_in[layer, tracer, :, piece]), preferred_element_type=F32
                    )
                )
            low_term = pltpu.roll(jnp.concatenate(lows, axis=1), 1, 1)
            high_term = pltpu.roll(jnp.concatenate(highs, axis=1), columns - 1, 1)
            g_out[layer, tracer] = (
                inv_denom * jnp.concatenate(solved, axis=1) - weight_low * low_term - weight_high * high_term
            )

    for layer in range(layers):
        step(layer)


def own_columns(place, k, width):
    return pl.ds(pl.multiple_of((place[0] ^ k) * width, width), width)


def meta_rows(meta, own, layers, layer):
    return [meta[i * layers + layer : i * layers + layer + 1, own] for i in range(4)]


def edge_value(fix, layer, tracer, tracers, side):
    lane = lax.broadcasted_iota(jnp.int32, (1, 128), 1)
    at = (2 * layer + side) * tracers + tracer
    return jnp.where(lane == (127 if side else 0), fix[:, at : at + 1], 0.0)


def with_edges(value, fix, layer, tracer, tracers, piece, columns):
    if piece.start == 0:
        low = value[:, :128] + edge_value(fix, layer, tracer, tracers, 0)
        value = jnp.concatenate([low, value[:, 128:]], axis=1)
    if piece.stop == columns:
        end = value.shape[1] - 128
        high = value[:, end:] + edge_value(fix, layer, tracer, tracers, 1)
        value = jnp.concatenate([value[:, :end], high], axis=1)
    return value


def local_forward_kernel(
    place, pair, cross, g_in, meta, sides, table, f_out, m0, m1, m2, m3
):
    layers, tracers, dofs, columns = g_in.shape
    odd = place[2] == 1
    from_low = pltpu.roll(jnp.where(odd, pair[...], cross[...]), 64, 1)
    from_high = pltpu.roll(jnp.where(odd, cross[...], pair[...]), tracers, 1)
    lane = lax.broadcasted_iota(jnp.int32, (1, 128), 1)
    halo = jnp.where(lane % (2 * tracers) < tracers, from_low, from_high)
    fix = -(sides[1:2, :] * typed(table[...], halo, kind_masks(sides[0:1, :], dofs)))
    for layer in range(layers):
        factor = meta[2 * layers + layer : 2 * layers + layer + 1, :]
        kinds = meta[3 * layers + layer : 3 * layers + layer + 1, :]
        for piece in pieces(columns):
            masks = kind_masks(kinds[:, piece], dofs)
            for tracer in range(tracers):
                value = with_edges(g_in[layer, tracer, :, piece], fix, layer, tracer, tracers, piece, columns)
                if layer > 0:
                    value = value - factor[:, piece] * typed(
                        table[...], f_out[layer - 1, tracer, :, piece], masks
                    )
                f_out[layer, tracer, :, piece] = value
    width = columns // MEMBERS
    top = tracers * dofs
    for k, target in enumerate((m0, m1, m2, m3)):
        own = pl.ds(pl.multiple_of((place[0] ^ k) * width, width), width)
        for tracer in range(tracers):
            target[tracer * dofs : (tracer + 1) * dofs, :] = f_out[layers - 1, tracer, :, own]
        target[top : top + 2 * layers, :] = meta[0 : 2 * layers, own]
        target[top + 2 * layers : top + 3 * layers, :] = meta[3 * layers : 4 * layers, own]
        if target.shape[0] > top + 3 * layers:
            target[top + 3 * layers :, :] = jnp.zeros((target.shape[0] - top - 3 * layers, width), F32)


def local_backward_kernel(
    place, f_in, meta, down, inverse, table, m0, m1, m2, m3, carried, downs, inv, sems
):
    copies = [
        pltpu.make_async_copy(source, target, sems.at[i])
        for i, (source, target) in enumerate(((down, downs), (inverse, inv)))
    ]
    for copy in copies:
        copy.start()
    for copy in copies:
        copy.wait()
    fold_table(inv, downs, table)
    layers, tracers, dofs, columns = f_in.shape
    for layer in reversed(range(layers)):
        scale, inv_denom, kinds = (meta[i * layers + layer : i * layers + layer + 1, :] for i in (0, 1, 3))
        for piece in pieces(columns):
            masks = kind_masks(kinds[:, piece], dofs)
            for tracer in range(tracers):
                solved = f_in[layer, tracer, :, piece]
                if layer < layers - 1:
                    solved = solved - inv_denom[:, piece] * carried[tracer, :, piece]
                carried[tracer, :, piece] = scale[:, piece] * typed(table[...], solved, masks)
    width = columns // MEMBERS
    for k, target in enumerate((m0, m1, m2, m3)):
        own = pl.ds(pl.multiple_of((place[0] ^ k) * width, width), width)
        for tracer in range(tracers):
            target[tracer * dofs : (tracer + 1) * dofs, :] = carried[tracer, :, own]


def chain_rows(block_ref, top, layers, layer):
    def row(which):
        at = top + which * layers + layer
        return block_ref[at : at + 1, :]

    return row(0), row(1), row(2)


def forward_chain(turn, layers, tracers, table, blocks, entering, held):
    rows = entering.shape[1]
    dofs = rows // tracers
    parts = [slice(r * dofs, (r + 1) * dofs) for r in range(tracers)]
    if turn == 0:
        held[0] = jnp.zeros(held.shape[1:], F32)
        entering[1] = blocks[0, 0:rows, :]

    def step(block, carry):
        values = [entering[block, here, :] for here in parts]
        for layer in range(layers):
            scale, inv_denom, kinds = chain_rows(blocks.at[block], rows, layers, layer)
            masks = kind_masks(kinds, dofs)
            factor = -(scale * inv_denom)
            values = [factor * typed(table[...], v, masks) for v in values]
            for value, here in zip(values, parts):
                held[block, layer, here, :] = value
        for value, here in zip(values, parts):
            entering[block + 1, here, :] = value + blocks[block, here, :]
        return carry

    lax.fori_loop(1 if turn == 0 else 0, MEMBERS, step, 0)


def backward_chain(turn, layers, tracers, table, blocks, terms, returning, held):
    rows = returning.shape[1]
    dofs = rows // tracers
    parts = [slice(r * dofs, (r + 1) * dofs) for r in range(tracers)]

    def step(index, carry):
        block = MEMBERS - 1 - index
        values = [returning[block + 1, here, :] for here in parts]
        for layer in reversed(range(layers)):
            scale, inv_denom, kinds = chain_rows(blocks.at[block], rows, layers, layer)
            masks = kind_masks(kinds, dofs)
            values = [
                scale * typed(table[...], held[block, layer, here, :] - inv_denom * value, masks)
                for value, here in zip(values, parts)
            ]
        for value, here in zip(values, parts):
            returning[block, here, :] = value + terms[block, here, :]
        return carry

    lax.fori_loop(0, MEMBERS - 1 if turn == 0 else MEMBERS, step, 0)


def take(place, sources, target, top=0):
    for k, source in enumerate(sources):
        target[place[0] ^ k, top:, :] = source[top:, :]


def give(place, targets, source, first):
    for k, target in enumerate(targets):
        target[...] = source[first + (place[0] ^ k)]


def chain_forward_kernel(turn, layers, tracers, place, inflow, table, *rest):
    if turn == 0:
        *messages, states, entering, outflow, blocks = rest
        take(place, messages, blocks)
    else:
        blocks, states, entering, outflow = rest

    @pl.when(place[1] == turn)
    def active():
        entering[0] = inflow[...] if turn > 0 else jnp.zeros(inflow.shape, F32)
        forward_chain(turn, layers, tracers, table, blocks, entering, states)
        outflow[...] = entering[MEMBERS]


def chain_last_kernel(
    turn, layers, tracers, place, inflow, up_table, down_table, blocks, e0, e1, e2, e3,
    entering, returning, outflow, terms, held,
):
    take(place, (e0, e1, e2, e3), terms)

    @pl.when(place[1] == turn)
    def active():
        entering[0] = inflow[...] if turn > 0 else jnp.zeros(inflow.shape, F32)
        forward_chain(turn, layers, tracers, up_table, blocks, entering, held)
        returning[MEMBERS] = jnp.zeros(inflow.shape, F32)
        backward_chain(turn, layers, tracers, down_table, blocks, terms, returning, held)
        outflow[...] = returning[0]


def chain_backward_kernel(turn, layers, tracers, place, inflow, table, blocks, terms, states, returning, outflow):
    @pl.when(place[1] == turn)
    def active():
        returning[MEMBERS] = inflow[...]
        backward_chain(turn, layers, tracers, table, blocks, terms, returning, states)
        outflow[...] = returning[0]


def chain_first_kernel(layers, tracers, place, inflow, table, blocks, terms, states, *rest):
    others, outs, returning = rest[: -MEMBERS - 1], rest[-MEMBERS - 1 : -1], rest[-1]

    @pl.when(place[1] == 0)
    def active():
        returning[MEMBERS] = inflow[...]
        backward_chain(0, layers, tracers, table, blocks, terms, returning, states)
        give(place, outs, returning, 1)

    give_kernel(1, 1, place, *others, *outs)


def give_kernel(first, turn, place, *rest):
    sources, outs = rest[:-MEMBERS], rest[-MEMBERS:]
    for at, source in enumerate(sources):
        @pl.when(place[1] == turn + at)
        def mine():
            give(place, outs, source, first)


def final_forward_kernel(place, f_in, meta, table, m0, m1, m2, m3, f_out, state):
    _, layers, tracers, dofs, width = f_out.shape
    for layer in range(layers):
        for k, message in enumerate((m0, m1, m2, m3)):
            own = own_columns(place, k, width)
            factor, kinds = meta_rows(meta, own, layers, layer)[2:]
            masks = kind_masks(kinds, dofs)
            for tracer in range(tracers):
                here = slice(tracer * dofs, (tracer + 1) * dofs)
                before = message[here, :] if layer == 0 else state[k, tracer]
                value = -(factor * typed(table[...], before, masks))
                f_out[k, layer, tracer] = f_in[layer, tracer, :, own] + value
                if layer < layers - 1:
                    state[k, tracer] = value


def final_backward_kernel(ks, place, f_in, meta, table, *rest):
    messages = rest[: len(ks)]
    out, carried, solved, sems = rest[-4:]
    _, layers, tracers, dofs, width = f_in.shape
    copies = []
    for layer in reversed(range(layers)):
        for i, (k, message) in enumerate(zip(ks, messages)):
            own = own_columns(place, k, width)
            scale, inv_denom, _, kinds = meta_rows(meta, own, layers, layer)
            masks = kind_masks(kinds, dofs)
            for tracer in range(tracers):
                here = slice(tracer * dofs, (tracer + 1) * dofs)
                before = message[here, :] if layer == layers - 1 else carried[i, tracer]
                solved[i, layer, tracer] = f_in[k, layer, tracer] - inv_denom * before
            copies.append(
                pltpu.make_async_copy(solved.at[i, layer], out.at[layer, :, :, own], sems.at[i, layer])
            )
            copies[-1].start()
            if layer > 0:
                for tracer in range(tracers):
                    carried[i, tracer] = scale * typed(table[...], solved[i, layer, tracer], masks)
    for copy in copies:
        copy.wait()


def per_device(rhs, lagged, kinds, stream, span, absorb, up, down, inverse):
    layers, tracers, dofs, columns = rhs.shape
    rows = tracers * dofs
    width = columns // MEMBERS
    count = lax.axis_size("stream")
    groups = count // MEMBERS
    position = lax.axis_index("stream")
    place = jnp.stack(
        [position % MEMBERS, position // MEMBERS, lax.axis_index("span") % 2]
    ).astype(jnp.int32)
    long_rows = rows + -(-3 * layers // 8) * 8
    vmem, anywhere, smem = (pl.BlockSpec(memory_space=s) for s in (pltpu.VMEM, pl.ANY, pltpu.SMEM))
    full = functools.partial(jax.ShapeDtypeStruct, dtype=F32)
    field = 4 * rhs.size
    product = 2 * KINDS * dofs * 3 * dofs * tracers * columns
    some = 12 << 20
    table_shape = (KINDS * dofs, 3 * dofs)
    fix = full((dofs, 128))

    def sent(value, k):
        return lax.ppermute(value, "stream", [(i, i ^ k) for i in range(count)]) if k else value

    def exchanged(messages):
        return [sent(value, k) for k, value in enumerate(messages)]

    def between(values, source, target):
        pairs = [(source * MEMBERS + i, target * MEMBERS + i) for i in range(MEMBERS)]
        return lax.ppermute(values, "stream", pairs)

    piece = (layers, tracers, dofs, width)
    early, late = tuple(range(MEMBERS - 1)), (MEMBERS - 1,)
    message = full((rows, width))
    long_message = full((long_rows, width))
    table = jax.ShapeDtypeStruct(table_shape, BF16)
    inputs = (rhs, lagged, kinds, stream, span, absorb, up, inverse)

    g, meta, sides, edges, up_table = pl.pallas_call(
        span_kernel,
        out_shape=(
            full(rhs.shape), full((4 * layers, columns)), full((8, 128)), fix, table,
        ),
        in_specs=[smem] + [anywhere] * len(inputs),
        out_specs=(vmem,) * 5,
        scratch_shapes=[pltpu.VMEM((dofs, 3 * dofs), BF16)]
        + [pltpu.VMEM(value.shape, value.dtype) for value in inputs]
        + [pltpu.SemaphoreType.DMA((2 * layers + 6,))],
        name="span_terms",
        **params(1 << 10, 1 << 10, some + 3 * field),
    )(place, *(pltpu.with_memory_space_constraint(value, pltpu.HBM) for value in inputs))

    across = lax.axis_size("span")
    crossing = [(i, i + 1) for i in range(1, across - 1, 2)]
    pair = lax.ppermute(edges, "span", [(i, i ^ 1) for i in range(across)])
    cross = lax.ppermute(edges, "span", crossing + [(b, a) for a, b in crossing])

    def piece_scratch(ks):
        return [pltpu.VMEM((len(ks), *piece), F32), pltpu.SemaphoreType.DMA((len(ks), layers))]

    f_zero, *out_b = pl.pallas_call(
        local_forward_kernel,
        out_shape=(full(rhs.shape),) + (long_message,) * MEMBERS,
        in_specs=[smem] + [vmem] * 6,
        out_specs=(vmem,) * (1 + MEMBERS),
        name="local_forward",
        **params(1 << 10, 1 << 10, some + field),
    )(place, pair, cross, g, meta, sides, up_table)
    in_b = exchanged(out_b)

    down_table, *out_e = pl.pallas_call(
        local_backward_kernel,
        out_shape=(table,) + (message,) * MEMBERS,
        in_specs=[smem] + [vmem] * 2 + [anywhere] * 2,
        out_specs=(vmem,) * (1 + MEMBERS),
        scratch_shapes=[
            pltpu.VMEM((tracers, dofs, columns), F32), pltpu.VMEM(down.shape, F32),
            pltpu.VMEM(inverse.shape, F32), pltpu.SemaphoreType.DMA((2,)),
        ],
        name="local_backward",
        **params(1 << 10, 1 << 10, some + field),
    )(place, f_zero, meta, *(pltpu.with_memory_space_constraint(value, pltpu.HBM) for value in (down, inverse)))
    in_e = exchanged(out_e)
    in_b, _ = lax.optimization_barrier((in_b, out_e))

    blocks = full((MEMBERS, long_rows, width))
    terms = full((MEMBERS, rows, width))
    flows = full((MEMBERS + 1, rows, width))
    held = (MEMBERS, layers, rows, width)
    inflow = out_e[0]
    states, entering, returning = [], [], []
    gathered = in_b
    for turn in range(groups - 1):
        state, entered, outflow, *block_values = pl.pallas_call(
            functools.partial(chain_forward_kernel, turn, layers, tracers),
            out_shape=(full(held), flows, message) + (blocks,) * (turn == 0),
            in_specs=[smem] + [vmem] * (2 + len(gathered)),
            out_specs=(vmem,) * (4 if turn == 0 else 3),
            name=f"chain_forward_{turn}",
            **params(layers * product, 2 * field, some + 2 * field),
        )(place, inflow, up_table, *gathered)
        if turn == 0:
            gathered = block_values
        states.append(state)
        entering.append(entered)
        inflow = between(outflow, turn, turn + 1)

    entered, returned, outflow, terms = pl.pallas_call(
        functools.partial(chain_last_kernel, groups - 1, layers, tracers),
        out_shape=(flows, flows, message, terms),
        in_specs=[smem] + [vmem] * (4 + MEMBERS),
        out_specs=(vmem,) * 4,
        scratch_shapes=[pltpu.VMEM(held, F32)],
        name="chain_last",
        **params(2 * layers * product, 2 * field, some + 2 * field),
    )(place, inflow, up_table, down_table, *gathered, *in_e)
    entering.append(entered)
    returning.insert(0, returned)
    out_f = pl.pallas_call(
        functools.partial(give_kernel, 0, 0),
        out_shape=(message,) * MEMBERS,
        in_specs=[smem] + [vmem] * groups,
        out_specs=(vmem,) * MEMBERS,
        name="give_forward",
        **params(1 << 10, 1 << 10, some),
    )(place, *entering)
    in_f = exchanged(out_f)

    for turn in reversed(range(1, groups - 1)):
        inflow = between(outflow, turn + 1, turn)
        returned, outflow = pl.pallas_call(
            functools.partial(chain_backward_kernel, turn, layers, tracers),
            out_shape=(flows, message),
            in_specs=[smem] + [vmem] * 5,
            out_specs=(vmem,) * 2,
            name=f"chain_backward_{turn}",
            **params(layers * product, 2 * field, some + field),
        )(place, inflow, down_table, *gathered, terms, states[turn])
        returning.insert(0, returned)
    inflow = between(outflow, 1, 0)
    out_h = pl.pallas_call(
        functools.partial(chain_first_kernel, layers, tracers),
        out_shape=(message,) * MEMBERS,
        in_specs=[smem] + [vmem] * (5 + len(returning)),
        out_specs=(vmem,) * MEMBERS,
        scratch_shapes=[pltpu.VMEM(flows.shape, F32)],
        name="chain_backward_0",
        **params(layers * product, 2 * field, some + field),
    )(place, inflow, down_table, *gathered, terms, states[0], *returning)
    in_h = exchanged(out_h)

    f_part = pl.pallas_call(
        final_forward_kernel,
        out_shape=full((MEMBERS, *piece)),
        in_specs=[smem] + [vmem] * (3 + MEMBERS),
        out_specs=vmem,
        scratch_shapes=[pltpu.VMEM((MEMBERS, tracers, dofs, width), F32)],
        name="final_forward",
        **params(1 << 10, 1 << 10, some + 2 * field),
    )(place, f_zero, meta, up_table, *in_f)
    out = ()
    for ks in (early, late):
        out = (
            pl.pallas_call(
                functools.partial(final_backward_kernel, ks),
                out_shape=full(rhs.shape),
                in_specs=[smem] + [vmem] * (3 + len(ks)) + [anywhere] * len(out),
                out_specs=anywhere,
                scratch_shapes=[pltpu.VMEM((len(ks), tracers, dofs, width), F32)] + piece_scratch(ks),
                input_output_aliases={4 + len(ks): 0} if out else {},
                name=f"final_backward_{ks[0]}",
                **params(1 << 10, 1 << 10, some + field),
            )(place, f_part, meta, down_table, *(in_h[k] for k in ks), *out),
        )
    return out[0]


def solution(mesh):
    return jax.shard_map(
        per_device,
        mesh=mesh,
        in_specs=(
            P("stream", None, None, "span"),
            P("stream", None, None, "span"),
            P(None, "stream", "span"),
            P("stream", "span"),
            P(None, "stream", "span"),
            P("stream", "span"),
            P(),
            P(),
            P(),
        ),
        out_specs=P("stream", None, None, "span"),
        check_vma=False,
    )
```
